128 devices in a mesh: grp: 16 (over y, z), sub: 8 (over x, core).
Axes of the slice: x: 4, y: 4, z: 4, core: 2. Of those that a mesh axis runs over, the one named last changes fastest.
Arguments:
- loads: float32 [1024, 256, 384], P(('grp', 'sub')), may hold values from -60 to 60
- diagonal_blocks: bfloat16 [1024, 384, 384], P(('grp', 'sub')), may hold values from -1 to 4
- lower_coupling: bfloat16 [1024, 384, 384], P(('grp', 'sub')), may hold values from -0.15625 to 0.15625
- upper_coupling: bfloat16 [1024, 384, 384], P(('grp', 'sub')), may hold values from -0.15625 to 0.15625
- local_inverse: bfloat16 [3, 1024, 384, 384], P(None, ('grp', 'sub')), may hold values from -0.5 to 1
- deflation: bfloat16 [1024, 32, 384], P(('grp', 'sub')), may hold values from -0.29882812 to 0.29882812
- coarse_inverse: float32 [4096, 4096], P(('grp', 'sub')), may hold values from -1 to 2, as said below
- coarse_order: int32 [4096], replicated, may hold values from 0 to 4095, as said below
Outputs:
- solution: float32 [1024, 256, 384], P(('grp', 'sub'))
- final_residual: float32 [1024, 256, 384], P(('grp', 'sub'))
- relative_residual: float32 [256], replicated
The draws below stay inside these ranges and needn't reach their ends.
Inputs may be any that keep to these rules, and one draw needn't show every extreme that they name: `coarse_order`: each of 0 to 4095 once. coarse_inverse with its columns put back in coarse numbering is symmetric.
All inputs are finite; a program needn't handle non-finite values.
Results may differ from the reference program's by a relative error of at most 0.008.
Values may be sent and summed in bfloat16 or wider, within the bound.
A program may use at most 128 MiB of HBM per device.

```python
import math
import jax
import jax.numpy as jnp
from jax import lax

L = 8
K = 256
W = 384
NDEF = 32
NL = 1024
NCOARSE = 4096


def shared_order(key):
    return jax.random.permutation(jax.random.fold_in(key, 17), NCOARSE).astype(jnp.int32)


def draw_coarse_order(key, part):
    return shared_order(key)


def draw_coarse_inverse(key, part):
    ordering = shared_order(key)
    key = jax.random.fold_in(key, 5)
    entries = jax.random.truncated_normal(key, -4.0, 4.0, (NCOARSE, NCOARSE))
    symmetric = (entries + entries.T) * (0.35 / math.sqrt(NCOARSE))
    identity = (jnp.arange(NCOARSE)[:, None] == jnp.arange(NCOARSE)[None, :]).astype(jnp.float32)
    return jnp.take(symmetric + 1.5 * identity, ordering, axis=1)


def draw_loads(key, part):
    key = jax.random.fold_in(key, 1)
    first_key, second_key, third_key = jax.random.split(key, 3)
    position = jnp.arange(NL, dtype=jnp.float32)
    rising = 0.5 + position / max(NL - 1, 1)
    plane_scale = rising * jnp.exp(jax.random.uniform(second_key, (NL,), minval=math.log(0.3), maxval=math.log(3.0)))
    unknown_scale = jnp.exp(jax.random.uniform(third_key, (W,), minval=math.log(0.3), maxval=math.log(3.0)))
    factor = plane_scale[:, None, None] * unknown_scale[None, None, :]
    random_part = jax.random.truncated_normal(first_key, -4.0, 4.0, (NL, K, W))
    return random_part * factor


def draw_diagonal_blocks(key, part):
    key = jax.random.fold_in(key, 2)
    first_key, second_key = jax.random.split(key, 2)
    diagonal = jax.random.uniform(first_key, (NL, W), minval=1.5, maxval=3.0)
    spread = jax.random.truncated_normal(second_key, -4.0, 4.0, (NL, W, W))
    identity = (jnp.arange(W)[:, None] == jnp.arange(W)[None, :]).astype(jnp.float32)
    return (spread * (0.6 / math.sqrt(W)) + identity[None] * diagonal[:, :, None]).astype(jnp.bfloat16)


def draw_local_inverse(key, part):
    key = jax.random.fold_in(key, 3)
    first_key, second_key = jax.random.split(key, 2)
    diagonal = jax.random.uniform(first_key, (NL, W), minval=0.3, maxval=0.6)
    spread = jax.random.truncated_normal(second_key, -4.0, 4.0, (3, NL, W, W))
    band_scale = jnp.array([0.25, 0.15, 0.25], jnp.float32) / math.sqrt(W)
    identity = (jnp.arange(W)[:, None] == jnp.arange(W)[None, :]).astype(jnp.float32)
    centre = (jnp.arange(3) == 1).astype(jnp.float32)
    leading = centre[:, None, None, None] * identity[None, None] * diagonal[None, :, :, None]
    return (spread * band_scale[:, None, None, None] + leading).astype(jnp.bfloat16)


def shard_levels(own_key, shape, shards, low, top_value):
    level = 1.0
    for dim, shards_of in shards:
        draws = jax.random.uniform(jax.random.fold_in(jax.random.fold_in(own_key, 6), dim), (shards_of,), jnp.float32, low / len(shards), top_value / len(shards))
        level = level * jnp.repeat(jnp.exp(draws), shape[dim] // shards_of).reshape((-1,) + (1,) * (len(shape) - 1 - dim))
    return level


def gaussian(stream_key, dims, scale, bound, cuts=(), held_as=jnp.bfloat16):
    drawn = jax.random.normal(stream_key, dims, jnp.float32) * scale
    if len(cuts) > 0:
        drawn = shard_levels(stream_key, dims, cuts, -0.22, 0.18) * drawn
    return jnp.clip(drawn, min=-bound, max=bound).astype(held_as)


def setup_inputs(seed: int = 0) -> dict:
    key_of = jax.random.split(jax.random.key(seed), 9)
    return {
        "loads": draw_loads(jax.random.fold_in(key_of[8], 71), 0),
        "diagonal_blocks": draw_diagonal_blocks(jax.random.fold_in(key_of[8], 71), 0),
        "lower_coupling": gaussian(key_of[2], (NL, W, W), (4 * W) ** -0.5, 0.15625, ((0, 128),)),
        "upper_coupling": gaussian(key_of[3], (NL, W, W), (4 * W) ** -0.5, 0.15625, ((0, 128),)),
        "local_inverse": draw_local_inverse(jax.random.fold_in(key_of[8], 71), 0),
        "deflation": gaussian(key_of[5], (NL, NDEF, W), 0.06, 0.29882812, ((0, 128),)),
        "coarse_inverse": draw_coarse_inverse(jax.random.fold_in(key_of[8], 71), 0),
        "coarse_order": draw_coarse_order(jax.random.fold_in(key_of[8], 71), 0),
    }


def banded_apply(rounded, left_blocks, centre_blocks, right_blocks):
    zero_plane = jnp.zeros((1, K, W), rounded.dtype)
    padded = jnp.concatenate([zero_plane, rounded, zero_plane], axis=0)
    groups = NL // L

    def one_block(operands):
        preceding, middle, following, left_part, centre_part, right_part = operands
        summed = jnp.einsum('lkw,lwv->lkv', preceding.astype(jnp.float32), left_part.astype(jnp.float32))
        summed = summed + jnp.einsum('lkw,lwv->lkv', middle.astype(jnp.float32), centre_part.astype(jnp.float32))
        return summed + jnp.einsum('lkw,lwv->lkv', following.astype(jnp.float32), right_part.astype(jnp.float32))
    members = (padded[:-2], rounded, padded[2:], left_blocks, centre_blocks, right_blocks)
    operands = tuple((member.reshape((groups, L) + member.shape[1:]) for member in members))
    return lax.map(one_block, operands).reshape(NL, K, W)

def precondition(field, local_inverse, deflation, coarse_inverse, coarse_order):
    rounded = field.astype(jnp.bfloat16)
    local_part = banded_apply(rounded, local_inverse[0], local_inverse[1], local_inverse[2])
    groups = NL // L

    def project_block(operands):
        vectors, values = operands
        return jnp.einsum('liw,lkw->ik', vectors.astype(jnp.float32), values.astype(jnp.float32))
    coefficients = lax.map(project_block, (deflation.reshape(groups, L, NDEF, W), rounded.reshape(groups, L, K, W)))
    coefficients = coefficients.reshape(NCOARSE, K)
    picked = jnp.take(coefficients, coarse_order, axis=0)
    solved = jnp.dot(coarse_inverse, picked, precision=lax.Precision.HIGHEST, preferred_element_type=jnp.float32)
    solved_half = solved.astype(jnp.bfloat16)

    def expand_block(operands):
        amounts, vectors = operands
        return jnp.einsum('ik,liw->lkw', amounts.astype(jnp.float32), vectors.astype(jnp.float32))
    coarse_part = lax.map(expand_block, (solved_half.reshape(groups, NDEF, K), deflation.reshape(groups, L, NDEF, W)))
    return local_part + coarse_part.reshape(NL, K, W)

def operate(field, diagonal_blocks, lower_coupling, upper_coupling):
    return banded_apply(field.astype(jnp.bfloat16), lower_coupling, diagonal_blocks, upper_coupling)

def inner(first, second):
    return lax.optimization_barrier(jnp.sum(first * second, axis=(0, 2)))

def reference(loads, diagonal_blocks, lower_coupling, upper_coupling, local_inverse, deflation, coarse_inverse, coarse_order):
    initial_norm = jnp.sqrt(inner(loads, loads))
    basis_one = loads / initial_norm[None, :, None]
    precond_one = precondition(basis_one, local_inverse, deflation, coarse_inverse, coarse_order)
    image_one = operate(precond_one, diagonal_blocks, lower_coupling, upper_coupling)
    entry_11 = inner(basis_one, image_one)
    remainder_one = image_one - entry_11[None, :, None] * basis_one
    entry_21 = jnp.sqrt(inner(remainder_one, remainder_one))
    basis_two = remainder_one / entry_21[None, :, None]
    precond_two = precondition(basis_two, local_inverse, deflation, coarse_inverse, coarse_order)
    image_two = operate(precond_two, diagonal_blocks, lower_coupling, upper_coupling)
    entry_12 = inner(basis_one, image_two)
    entry_22 = inner(basis_two, image_two)
    remainder_two = image_two - entry_12[None, :, None] * basis_one - entry_22[None, :, None] * basis_two
    entry_32 = jnp.sqrt(inner(remainder_two, remainder_two))
    minor_12 = entry_11 * entry_22 - entry_21 * entry_12
    minor_13 = entry_11 * entry_32
    minor_23 = entry_21 * entry_32
    determinant = minor_12 * minor_12 + minor_13 * minor_13 + minor_23 * minor_23
    gram_11 = entry_11 * entry_11 + entry_21 * entry_21
    gram_12 = entry_11 * entry_12 + entry_21 * entry_22
    gram_22 = entry_12 * entry_12 + entry_22 * entry_22 + entry_32 * entry_32
    right_one = initial_norm * entry_11
    right_two = initial_norm * entry_12
    weight_one = (gram_22 * right_one - gram_12 * right_two) / determinant
    weight_two = (gram_11 * right_two - gram_12 * right_one) / determinant
    solution = weight_one[None, :, None] * precond_one + weight_two[None, :, None] * precond_two
    final_residual = loads - weight_one[None, :, None] * image_one - weight_two[None, :, None] * image_two
    error_one = initial_norm - entry_11 * weight_one - entry_12 * weight_two
    error_two = -(entry_21 * weight_one + entry_22 * weight_two)
    error_three = -entry_32 * weight_two
    relative_residual = (error_one * error_one + error_two * error_two + error_three * error_three) / (initial_norm * initial_norm)
    return (solution, final_residual, relative_residual)
```

```python
import jax
import jax.numpy as jnp
from jax import lax
from jax.experimental import pallas as pl
from jax.experimental.pallas import tpu as pltpu
from jax.sharding import PartitionSpec as P

MESH = pl.DeviceIdType.MESH
F32 = jnp.float32
BF16 = jnp.bfloat16

L = 8
K = 256
W = 384
NDEF = 32
SIDE = 4
SAME = SIDE * SIDE * SIDE * NDEF
NCOARSE = 2 * SAME
BAND = 3 * W
GATHER_PARTS = (
    ("xyz", 0, 16, 0, 256),
    ("yzx", 16, 32, 0, 128),
    ("zxy", 16, 32, 128, 256),
)


def lanes(plane):
    return pl.ds(pl.multiple_of(plane * W, W), W)


def kernel(
    loads_h, diagonal_h, lower_h, upper_h, local_h, deflation_h, inverse_h, order_h,
    solution_h, residual_h, relative_ref,
    v0, z0, u0, z1, u1, field0, field1, field2, field3, precond, coupling, vectors,
    own_rows, other_rows, split_rows, columns, order, place, gathered, partial, other_partial,
    gram, sums, slots,
    load_sem, vector_sem, block_sem, row_sem, out_sem,
    halo_send, halo_recv, gather_send, gather_recv, row_send, row_recv,
    partial_send, partial_recv, sum_send, sum_recv,
):
    grp = lax.axis_index("grp")
    sub = lax.axis_index("sub")
    y, z, x, core = grp // SIDE, grp % SIDE, sub // 2, sub % 2
    me = grp * 8 + sub
    before = (me + 127) % 128
    after = (me + 1) % 128
    before_id = (before // 8, before % 8)
    after_id = (after // 8, after % 8)
    core_id = (grp, x * 2 + 1 - core)
    place_of = {"x": x, "y": y, "z": z}

    def partner(axis, step):
        if axis == "x":
            return (grp, ((x + step) % SIDE) * 2 + core)
        if axis == "y":
            return (((y + step) % SIDE) * SIDE + z, sub)
        return (y * SIDE + (z + step) % SIDE, sub)

    def load_copy(plane):
        return pltpu.make_async_copy(loads_h.at[plane], v0.at[plane], load_sem.at[plane])

    def vector_copy(plane):
        return pltpu.make_async_copy(
            deflation_h.at[plane], vectors.at[:NDEF, lanes(plane)], vector_sem.at[plane]
        )

    block_copies = [
        pltpu.make_async_copy(source, target, block_sem.at[i])
        for i, (source, target) in enumerate([
            (local_h.at[0], precond.at[:, 0]),
            (local_h.at[1], precond.at[:, 1]),
            (local_h.at[2], precond.at[:, 2]),
            (lower_h, coupling.at[:, 0]),
            (diagonal_h, coupling.at[:, 1]),
            (upper_h, coupling.at[:, 2]),
        ])
    ]
    row_copy = pltpu.make_async_copy(inverse_h, own_rows, row_sem.at[0])
    order_copy = pltpu.make_async_copy(order_h, order, row_sem.at[1])
    for plane in (0, 7, 1, 2, 3, 4, 5, 6):
        load_copy(plane).start()
    for plane in range(L):
        vector_copy(plane).start()
    row_copy.start()
    order_copy.start()
    for copy in block_copies:
        copy.start()

    barrier = pltpu.get_barrier_semaphore()
    partners = [partner(axis, step) for axis in "xyz" for step in (1, 2, 3)]
    partners += [core_id, before_id, after_id]
    for device in partners:
        pl.semaphore_signal(barrier, inc=1, device_id=device, device_id_type=MESH)
    pl.semaphore_wait(barrier, len(partners))

    def remote(source, target, send, recv, device):
        return pltpu.make_async_remote_copy(
            src_ref=source, dst_ref=target, send_sem=send, recv_sem=recv,
            device_id=device, device_id_type=MESH,
        )

    row_exchange = remote(inverse_h, other_rows, row_send.at[0], row_recv.at[0], core_id)
    row_exchange.start()

    sends = [row_exchange]

    def halo_copies(field, which):
        return (
            remote(
                field.at[:, lanes(1)], field.at[:, lanes(L + 1)],
                halo_send.at[which, 0], halo_recv.at[which, 0], before_id,
            ),
            remote(
                field.at[:, lanes(L)], field.at[:, lanes(0)],
                halo_send.at[which, 1], halo_recv.at[which, 1], after_id,
            ),
        )

    def start_halo(field, which):
        for copy in halo_copies(field, which):
            copy.start()
            sends.append(copy)

    def finish_halo(field, which):
        for copy in halo_copies(field, which):
            copy.wait_recv()

        @pl.when(me == 0)
        def _():
            field[:, lanes(0)] = jnp.zeros((K, W), BF16)

        @pl.when(me == 127)
        def _():
            field[:, lanes(L + 1)] = jnp.zeros((K, W), BF16)

    def gather_copies(which, stage):
        found = []
        for part, (axes, row0, row1, lane0, lane1) in enumerate(GATHER_PARTS):
            done = axes[:stage]
            spot = tuple(slice(None) if name in done else place_of[name] for name in "yzx")
            block = gathered.at[(which,) + spot + (slice(row0, row1), slice(lane0, lane1))]
            for step in (1, 2, 3):
                found.append(remote(
                    block, block,
                    gather_send.at[which, part, stage, step - 1],
                    gather_recv.at[which, part, stage, step - 1],
                    partner(axes[stage], step),
                ))
        return found

    def start_gather(which, stage):
        copies = gather_copies(which, stage)
        for copy in copies:
            copy.start()
        sends.extend(copies)

    def finish_gather(which, stage):
        for copy in gather_copies(which, stage):
            copy.wait_recv()

    def coefficients(field, which):
        own = lax.dot_general(
            vectors[:NDEF], field[:, W:(L + 1) * W], (((1,), (1,)), ((), ())),
            preferred_element_type=F32,
        )
        gathered[which, y, z, x] = own.astype(BF16)

    def banded(field, blocks, plane):
        window = field[:, pl.ds(pl.multiple_of(plane * W, W), BAND)]
        return jnp.dot(
            window, blocks[plane].reshape(BAND, W), preferred_element_type=F32
        )

    def coarse_part(amounts, plane):
        return lax.dot_general(
            amounts, vectors[:, lanes(plane)], (((0,), (0,)), ((), ())),
            preferred_element_type=F32,
        )

    def finish_coarse(which):
        product = jnp.dot(
            columns[...], gathered[which].reshape(SAME, K), preferred_element_type=F32
        )
        both = product[:2 * NDEF] + product[2 * NDEF:]
        partial[which] = both
        exchange = remote(
            partial.at[which, NDEF:], other_partial.at[which],
            partial_send.at[which], partial_recv.at[which], core_id,
        )
        exchange.start()
        sends.append(exchange)
        exchange.wait_recv()
        total = partial[which, :NDEF] + other_partial[which]
        high = total.astype(BF16)
        low = (total - high.astype(F32)).astype(BF16)
        return jnp.concatenate([high, low], axis=0)

    def edge(i):
        return i * (L - 1)

    def round_load(plane):
        load_copy(plane).wait()
        field0[:, lanes(plane + 1)] = v0[plane].astype(BF16)

    round_load(0)
    round_load(7)
    start_halo(field0, 0)

    @pl.loop(1, L - 1)
    def _(plane):
        round_load(plane)

    @pl.loop(0, L)
    def _(plane):
        vector_copy(plane).wait()

    coefficients(field0, 0)
    start_gather(0, 0)
    vectors[NDEF:] = vectors[:NDEF]

    row_copy.wait()
    order_copy.wait()
    row_exchange.wait_recv()
    for i, rows in enumerate((own_rows, other_rows)):
        value = rows[...]
        high = value.astype(BF16)
        split_rows[i * NDEF:(i + 1) * NDEF] = high
        split_rows[(2 + i) * NDEF:(3 + i) * NDEF] = (value - high.astype(F32)).astype(BF16)
    unknown = order[...]
    chip, inside = unknown // (2 * NDEF), unknown % (2 * NDEF)
    mine = inside // NDEF == core
    place[...] = jnp.where(mine, chip * NDEF + inside % NDEF, -1)

    @pl.loop(0, SAME // 256)
    def _(block):
        base = block * 256
        total = jnp.zeros((4 * NDEF, 256), F32)
        for part in range(4):
            span = slice(part * 1024, (part + 1) * 1024)
            row = lax.broadcasted_iota(jnp.int32, (256, 1024), 0)
            hot = jnp.where(place[:, span] - base == row, 1.0, 0.0).astype(BF16)
            total += lax.dot_general(
                split_rows[:, span], hot, (((1,), (1,)), ((), ())), preferred_element_type=F32
            )
        columns[:, pl.ds(pl.multiple_of(base, 256), 256)] = total.astype(BF16)

    finish_gather(0, 0)
    start_gather(0, 1)
    for copy in block_copies[:3]:
        copy.wait()

    def precondition(field, result, which):
        @pl.loop(1, L - 1)
        def _(plane):
            result[plane] = banded(field, precond, plane)

        finish_gather(which, 1)
        start_gather(which, 2)
        finish_halo(field, which * 2)

        @pl.loop(0, 2)
        def _(i):
            result[edge(i)] = banded(field, precond, edge(i))

    def expand(result, field, which):
        finish_gather(which, 2)
        amounts = finish_coarse(which)

        def add(plane):
            total = result[plane] + coarse_part(amounts, plane)
            result[plane] = total
            field[:, lanes(plane + 1)] = total.astype(BF16)

        @pl.loop(0, 2)
        def _(i):
            add(edge(i))

        start_halo(field, which * 2 + 1)

        @pl.loop(1, L - 1)
        def _(plane):
            add(plane)

    def operate(field, result, which, rounded):
        def apply(plane):
            image = banded(field, coupling, plane)
            result[plane] = image
            if rounded is not None:
                rounded[:, lanes(plane + 1)] = image.astype(BF16)

        @pl.loop(1, L - 1)
        def _(plane):
            apply(plane)

        finish_halo(field, which * 2 + 1)

        @pl.loop(0, 2)
        def _(i):
            apply(edge(i))

    def inner_products(pairs):
        rows = 32

        @pl.loop(0, K // rows)
        def _(chunk):
            span = pl.ds(pl.multiple_of(chunk * rows, rows), rows)
            for column, first, second in pairs:
                total = jnp.zeros((rows, 128), F32)
                for plane in range(L):
                    for lane in range(0, W, 128):
                        total += (
                            first[plane, span, lane:lane + 128]
                            * second[plane, span, lane:lane + 128]
                        )
                gram[span, column:column + 1] = jnp.sum(total, axis=1, keepdims=True)

    precondition(field0, z0, 0)
    expand(z0, field1, 0)
    for copy in block_copies[3:]:
        copy.wait()
    operate(field1, u0, 0, field2)
    start_halo(field2, 2)
    coefficients(field2, 1)
    start_gather(1, 0)
    gram[...] = jnp.zeros((K, 128), F32)
    inner_products(((0, v0, v0), (1, v0, u0), (2, u0, u0)))
    finish_gather(1, 0)
    start_gather(1, 1)
    precondition(field2, z1, 1)
    expand(z1, field3, 1)
    operate(field3, u1, 1, None)
    inner_products(((3, v0, u1), (4, u0, u1), (5, u1, u1)))
    sums[...] = jnp.transpose(gram[...])[:8]

    pair = remote(sums, slots.at[0, 0], sum_send.at[0, 0], sum_recv.at[0, 0], core_id)
    pair.start()
    pair.wait()
    sums[...] = sums[...] + slots[0, 0]
    for stage, axis in ((1, "x"), (2, "y"), (3, "z")):
        spot = place_of[axis]
        slots[stage, spot] = sums[...]
        copies = [
            remote(
                slots.at[stage, spot], slots.at[stage, spot],
                sum_send.at[stage, step - 1], sum_recv.at[stage, step - 1],
                partner(axis, step),
            )
            for step in (1, 2, 3)
        ]
        for copy in copies:
            copy.start()
        for copy in copies:
            copy.wait()
        sums[...] = (slots[stage, 0] + slots[stage, 1]) + (slots[stage, 2] + slots[stage, 3])

    g00, g01, g11 = sums[0:1], sums[1:2], sums[2:3]
    g02, g12, g22 = sums[3:4], sums[4:5], sums[5:6]
    s0, s1, s2 = jnp.sqrt(g00), jnp.sqrt(g11), jnp.sqrt(g22)
    r01 = g01 / s0 / s1
    r02 = g02 / s0 / s2
    r11 = jnp.sqrt((1.0 - r01) * (1.0 + r01))
    r12 = (g12 / s1 / s2 - r01 * r02) / r11
    r22 = jnp.sqrt((1.0 - r02) * (1.0 + r02) - r12 * r12)
    n0 = r11 * r22
    n1 = r01 * r22
    n2 = r01 * r12 - r11 * r02
    share = n0 / (n0 * n0 + n1 * n1 + n2 * n2)
    relative_ref[...] = n0 * share
    scaled1 = -(share * n2) / r22
    weight1 = scaled1 * (s0 / s2)
    weight0 = (share * n1 - scaled1 * r12) / r11 * (s0 / s1)
    gram[...] = jnp.transpose(
        jnp.concatenate([weight0, weight1, jnp.zeros((126, K), F32)], axis=0)
    )

    def solution_copy(plane):
        return pltpu.make_async_copy(z0.at[plane], solution_h.at[plane], out_sem.at[0, plane])

    def residual_copy(plane):
        return pltpu.make_async_copy(v0.at[plane], residual_h.at[plane], out_sem.at[1, plane])

    @pl.loop(0, L)
    def _(plane):
        first = gram[:, 0:1]
        second = gram[:, 1:2]
        z0[plane] = first * z0[plane] + second * z1[plane]
        solution_copy(plane).start()
        v0[plane] = v0[plane] - first * u0[plane] - second * u1[plane]
        residual_copy(plane).start()

    for copy in sends:
        copy.wait_send()

    @pl.loop(0, L)
    def _(plane):
        solution_copy(plane).wait()
        residual_copy(plane).wait()


def local(
    loads, diagonal_blocks, lower_coupling, upper_coupling, local_inverse, deflation,
    coarse_inverse, coarse_order,
):
    hbm = pl.BlockSpec(memory_space=pl.ANY)
    field = pltpu.VMEM((L, K, W), F32)
    padded = pltpu.VMEM((K, (L + 2) * W), BF16)
    blocks = pltpu.VMEM((L, 3, W, W), BF16)
    dma = pltpu.SemaphoreType.DMA
    answer, residual, relative = pl.pallas_call(
        kernel,
        out_shape=(
            jax.ShapeDtypeStruct((L, K, W), F32),
            jax.ShapeDtypeStruct((L, K, W), F32),
            jax.ShapeDtypeStruct((1, K), F32),
        ),
        in_specs=[hbm] * 8,
        out_specs=(hbm, hbm, pl.BlockSpec(memory_space=pltpu.VMEM)),
        scratch_shapes=[
            field, field, field, field, field,
            padded, padded, padded, padded,
            blocks, blocks,
            pltpu.VMEM((2 * NDEF, L * W), BF16),
            pltpu.VMEM((NDEF, NCOARSE), F32),
            pltpu.VMEM((NDEF, NCOARSE), F32),
            pltpu.VMEM((4 * NDEF, NCOARSE), BF16),
            pltpu.VMEM((4 * NDEF, SAME), BF16),
            pltpu.VMEM((1, NCOARSE), jnp.int32),
            pltpu.VMEM((1, NCOARSE), jnp.int32),
            pltpu.VMEM((2, SIDE, SIDE, SIDE, NDEF, K), BF16),
            pltpu.VMEM((2, 2 * NDEF, K), F32),
            pltpu.VMEM((2, NDEF, K), F32),
            pltpu.VMEM((K, 128), F32),
            pltpu.VMEM((8, K), F32),
            pltpu.VMEM((4, SIDE, 8, K), F32),
            dma((L,)), dma((L,)), dma((6,)), dma((2,)), dma((2, L)),
            dma((4, 2)), dma((4, 2)), dma((2, 3, 3, 3)), dma((2, 3, 3, 3)),
            dma((1,)), dma((1,)), dma((2,)), dma((2,)), dma((4, 3)), dma((4, 3)),
        ],
        compiler_params=pltpu.CompilerParams(
            collective_id=0, has_side_effects=True, vmem_limit_bytes=60 * 2**20
        ),
        cost_estimate=pl.CostEstimate(
            flops=8 * 10**9, bytes_accessed=25 * 10**6, transcendentals=0
        ),
    )(
        loads, diagonal_blocks, lower_coupling, upper_coupling, local_inverse, deflation,
        coarse_inverse, coarse_order.reshape(1, NCOARSE),
    )
    return answer, residual, relative.reshape(K)


def solution(mesh):
    spread = P(("grp", "sub"))
    return jax.shard_map(
        local,
        mesh=mesh,
        in_specs=(
            spread, spread, spread, spread, P(None, ("grp", "sub")), spread, spread, P(),
        ),
        out_specs=(spread, spread, P()),
        check_vma=False,
    )
```

```python
import jax
import jax.numpy as jnp
from jax import lax
from jax.experimental import pallas as pl
from jax.experimental.pallas import tpu as pltpu
from jax.sharding import PartitionSpec as P

MESH = pl.DeviceIdType.MESH
F32 = jnp.float32
BF16 = jnp.bfloat16

L = 8
K = 256
W = 384
NDEF = 32
SIDE = 4
DEVICES = 128
SAME = SIDE * SIDE * SIDE * NDEF
NCOARSE = 2 * SAME
BAND = 3 * W
IMAGE_SCALE = 2.0 ** -24
GATHER_PARTS = (
    ("xyz", 0, 16, 0, 256),
    ("yzx", 16, 32, 0, 128),
    ("zxy", 16, 32, 128, 256),
)
NN = (((1,), (0,)), ((), ()))
NT = (((1,), (1,)), ((), ()))


def lanes(plane):
    return pl.ds(pl.multiple_of(plane * W, W), W)


def dot(first, second, form=NN, precision=None):
    return lax.dot_general(
        first, second, form, precision=precision, preferred_element_type=F32
    )


def two_terms(value):
    high = value.astype(BF16)
    return high, (value - high.astype(F32)).astype(BF16)


def kernel(
    loads_h, diagonal_h, lower_h, upper_h, local_h, deflation_h, inverse_h, order_h,
    solution_h, residual_h, relative_ref,
    v0, z0, u0, z1, u1, field0, field1, field2, field3, precond, coupling,
    padded_vectors, edge_vectors, expansion, images, image_coupling,
    own_rows, other_rows, split_rows, columns, order, place, gathered, own_low,
    partial, other_partial, coarse, amounts, projected, gram, sums, slots,
    load_sem, vector_sem, block_sem, row_sem, out_sem,
    halo_send, halo_recv, gather_send, gather_recv, row_send, row_recv,
    edge_send, edge_recv, column_send, column_recv,
    partial_send, partial_recv, sum_send, sum_recv,
):
    grp = lax.axis_index("grp")
    sub = lax.axis_index("sub")
    y, z, x, core = grp // SIDE, grp % SIDE, sub // 2, sub % 2
    me = grp * 8 + sub
    place_of = {"x": x, "y": y, "z": z}

    def along_chain(step):
        device = (me + step + DEVICES) % DEVICES
        return (device // 8, device % 8)

    before_id, after_id = along_chain(-1), along_chain(1)
    chip_before_id, chip_after_id = along_chain(-2), along_chain(2)
    core_id = (grp, x * 2 + 1 - core)

    def chip(at_x, at_y, at_z):
        return (at_y * SIDE + at_z, at_x * 2 + core)

    def partner(axis, step):
        spot = dict(place_of)
        spot[axis] = (spot[axis] + step) % SIDE
        return chip(spot["x"], spot["y"], spot["z"])

    z_low, z_high = z % 2, z // 2
    sum_groups = (
        (z_low * SIDE + x, [
            chip((x + step) % SIDE, y, 2 * z_high + (z_low + flip) % 2)
            for flip in (0, 1) for step in range(SIDE) if flip or step
        ]),
        (z_high * SIDE + y, [
            chip(x, (y + step) % SIDE, 2 * ((z_high + flip) % 2) + z_low)
            for flip in (0, 1) for step in range(SIDE) if flip or step
        ]),
    )

    def load_copy(plane):
        return pltpu.make_async_copy(loads_h.at[plane], v0.at[plane], load_sem.at[plane])

    def vector_copy(plane):
        return pltpu.make_async_copy(
            deflation_h.at[plane], padded_vectors.at[NDEF:2 * NDEF, lanes(plane + 1)],
            vector_sem.at[plane],
        )

    block_copies = [
        pltpu.make_async_copy(source, target, block_sem.at[i])
        for i, (source, target) in enumerate([
            (local_h.at[0], precond.at[:, 0]),
            (local_h.at[1], precond.at[:, 1]),
            (local_h.at[2], precond.at[:, 2]),
            (lower_h, coupling.at[:, 0]),
            (diagonal_h, coupling.at[:, 1]),
            (upper_h, coupling.at[:, 2]),
        ])
    ]
    row_copy = pltpu.make_async_copy(inverse_h, own_rows, row_sem.at[0])
    order_copy = pltpu.make_async_copy(order_h, order, row_sem.at[1])
    for plane in (0, 7, 1, 2, 3, 4, 5, 6):
        load_copy(plane).start()
    for plane in range(L):
        vector_copy(plane).start()
    row_copy.start()
    order_copy.start()

    barrier = pltpu.get_barrier_semaphore()
    partners = [partner(axis, step) for axis in "xyz" for step in (1, 2, 3)]
    partners += [core_id, before_id, after_id, chip_before_id, chip_after_id]
    partners += sum_groups[0][1] + sum_groups[1][1]
    for device in partners:
        pl.semaphore_signal(barrier, inc=1, device_id=device, device_id_type=MESH)

    padded_vectors[:NDEF] = jnp.zeros((NDEF, (L + 2) * W), BF16)
    padded_vectors[2 * NDEF:] = jnp.zeros((NDEF, (L + 2) * W), BF16)
    padded_vectors[NDEF:2 * NDEF, :W] = jnp.zeros((NDEF, W), BF16)
    padded_vectors[NDEF:2 * NDEF, (L + 1) * W:] = jnp.zeros((NDEF, W), BF16)
    expansion[...] = jnp.zeros((2 * 128, L * W), BF16)
    images[...] = jnp.zeros((3 * 128, L * W), BF16)
    own_low[...] = jnp.zeros((2, SIDE * NDEF, K), BF16)
    gram[...] = jnp.zeros((K, 128), F32)
    projected[...] = jnp.zeros((NDEF, K), F32)
    coarse[...] = jnp.zeros((128, K), F32)

    pl.semaphore_wait(barrier, len(partners))

    sends = []

    def remote(source, target, send, recv, device):
        return pltpu.make_async_remote_copy(
            src_ref=source, dst_ref=target, send_sem=send, recv_sem=recv,
            device_id=device, device_id_type=MESH,
        )

    def start(copies):
        for copy in copies:
            copy.start()
        sends.extend(copies)

    def received(copies):
        for copy in copies:
            copy.wait_recv()

    row_exchange = [
        remote(inverse_h, other_rows, row_send.at[0], row_recv.at[0], core_id)
    ]
    edge_exchange = [
        remote(
            deflation_h.at[0], edge_vectors.at[1], edge_send.at[0], edge_recv.at[0], before_id
        ),
        remote(
            deflation_h.at[L - 1], edge_vectors.at[0], edge_send.at[1], edge_recv.at[1], after_id
        ),
    ]
    column_exchange = [
        remote(
            columns.at[row:row + NDEF], columns.at[target:target + NDEF],
            column_send.at[i], column_recv.at[i], device,
        )
        for i, (row, target, device) in enumerate([
            (2 * NDEF, 0, chip_after_id),
            (6 * NDEF, 4 * NDEF, chip_after_id),
            (NDEF, 3 * NDEF, chip_before_id),
            (5 * NDEF, 7 * NDEF, chip_before_id),
        ])
    ]

    def halo_copies(field, which):
        return [
            remote(
                field.at[:, lanes(1)], field.at[:, lanes(L + 1)],
                halo_send.at[which, 0], halo_recv.at[which, 0], before_id,
            ),
            remote(
                field.at[:, lanes(L)], field.at[:, lanes(0)],
                halo_send.at[which, 1], halo_recv.at[which, 1], after_id,
            ),
        ]

    def start_halo(field, which):
        start(halo_copies(field, which))

    def finish_halo(field, which):
        received(halo_copies(field, which))

        @pl.when(me == 0)
        def _():
            field[:, lanes(0)] = jnp.zeros((K, W), BF16)

        @pl.when(me == DEVICES - 1)
        def _():
            field[:, lanes(L + 1)] = jnp.zeros((K, W), BF16)

    def gather_copies(which, stage):
        found = []
        for part, (axes, row0, row1, lane0, lane1) in enumerate(GATHER_PARTS):
            done = axes[:stage]
            spot = tuple(slice(None) if name in done else place_of[name] for name in "yzx")
            block = gathered.at[(which,) + spot + (slice(row0, row1), slice(lane0, lane1))]
            for step in (1, 2, 3):
                found.append(remote(
                    block, block,
                    gather_send.at[which, part, stage, step - 1],
                    gather_recv.at[which, part, stage, step - 1],
                    partner(axes[stage], step),
                ))
        return found

    def start_gather(which, stage):
        start(gather_copies(which, stage))

    def finish_gather(which, stage):
        received(gather_copies(which, stage))

    def share_coefficients(own, which):
        high, low = two_terms(own)
        gathered[which, y, z, x] = high
        start_gather(which, 0)
        own_low[which, pl.ds(pl.multiple_of(x * NDEF, NDEF), NDEF)] = low

    def banded(field, blocks, plane):
        window = field[:, pl.ds(pl.multiple_of(plane * W, W), BAND)]
        return dot(window, blocks[plane].reshape(BAND, W))

    def edge(i):
        return i * (L - 1)

    def finish_coarse(which):
        product = dot(columns[...], gathered[which].reshape(SAME, K))
        window = pl.ds(pl.multiple_of((y * SIDE + z) * 128, 128), 128)
        fix = dot(columns[:4 * NDEF, window], own_low[which])
        partial[which] = product[:4 * NDEF] + (product[4 * NDEF:] + fix)
        exchange = [remote(
            partial.at[which, pl.ds(pl.multiple_of((1 - core) * NDEF, NDEF), 3 * NDEF)],
            other_partial.at[which], partial_send.at[which], partial_recv.at[which], core_id,
        )]
        start(exchange)
        received(exchange)
        coarse[:3 * NDEF] = (
            partial[which, pl.ds(pl.multiple_of(core * NDEF, NDEF), 3 * NDEF)]
            + other_partial[which]
        )
        high, low = two_terms(jnp.transpose(coarse[...]))
        amounts[which, :, :128] = high
        amounts[which, :, 128:256] = low
        amounts[which, :, 256:] = high

    def precondition(field, result, rounded, which):
        def apply(plane):
            value = banded(field, precond, plane)
            result[plane] = value
            rounded[:, lanes(plane + 1)] = value.astype(BF16)

        finish_halo(field, 2 * which)

        @pl.loop(0, 2)
        def _(i):
            apply(edge(i))

        start_halo(rounded, 2 * which + 1)

        @pl.loop(1, L - 1)
        def _(plane):
            apply(plane)

    def operate(field, result, which, planes, project):
        @pl.loop(*planes)
        def _(i):
            plane = i if planes == (1, L - 1) else edge(i)
            image = banded(field, coupling, plane)
            result[plane] = image
            if project:
                projected[...] += dot(
                    padded_vectors[NDEF:2 * NDEF, lanes(plane + 1)], image.astype(BF16), NT
                )

    def add_image(result, rounded, plane, which):
        total = result[plane] + dot(amounts[which], images[:, lanes(plane)])
        result[plane] = total
        if rounded is not None:
            rounded[:, lanes(plane + 1)] = total.astype(BF16)

    def add_expansion(result, which):
        @pl.loop(0, L)
        def _(plane):
            result[plane] += dot(amounts[which, :, :256], expansion[:, lanes(plane)])

    def inner_products(pairs):
        rows = 32

        @pl.loop(0, K // rows)
        def _(chunk):
            span = pl.ds(pl.multiple_of(chunk * rows, rows), rows)
            for column, first, second in pairs:
                total = jnp.zeros((rows, 128), F32)
                for plane in range(L):
                    for lane in range(0, W, 128):
                        one = first[plane, span, lane:lane + 128]
                        two = second[plane, span, lane:lane + 128]
                        if first is u1:
                            one = one * IMAGE_SCALE
                        if second is u1:
                            two = two * IMAGE_SCALE
                        total += one * two
                gram[span, column:column + 1] = jnp.sum(total, axis=1, keepdims=True)

    def permute_columns(first, last):
        @pl.loop(first, last)
        def _(block):
            base = block * 256
            total = jnp.zeros((4 * NDEF, 256), F32)
            for part in range(4):
                span = slice(part * 1024, (part + 1) * 1024)
                row = lax.broadcasted_iota(jnp.int32, (256, 1024), 0)
                hot = jnp.where(place[:, span] - base == row, 1.0, 0.0).astype(BF16)
                total += dot(split_rows[:, span], hot, NT)
            target = pl.ds(pl.multiple_of(base, 256), 256)
            columns[NDEF:3 * NDEF, target] = total[:2 * NDEF].astype(BF16)
            columns[5 * NDEF:7 * NDEF, target] = total[2 * NDEF:].astype(BF16)

    start(row_exchange)
    start(edge_exchange)

    def round_load(plane):
        load_copy(plane).wait()
        field0[:, lanes(plane + 1)] = v0[plane].astype(BF16)

    round_load(0)
    round_load(L - 1)
    start_halo(field0, 0)

    @pl.loop(1, L - 1)
    def _(plane):
        round_load(plane)

    @pl.loop(0, L)
    def _(plane):
        vector_copy(plane).wait()

    for copy in block_copies:
        copy.start()

    share_coefficients(
        dot(padded_vectors[NDEF:2 * NDEF, W:(L + 1) * W], field0[:, W:(L + 1) * W], NT), 0
    )

    row_copy.wait()
    order_copy.wait()
    received(row_exchange)
    for rows, owner in ((own_rows, core), (other_rows, 1 - core)):
        high, low = two_terms(rows[...])
        split_rows[pl.ds(pl.multiple_of(owner * NDEF, NDEF), NDEF)] = high
        split_rows[pl.ds(pl.multiple_of((2 + owner) * NDEF, NDEF), NDEF)] = low
    unknown = order[...]
    inside = unknown % (2 * NDEF)
    place[...] = jnp.where(
        inside // NDEF == core, unknown // (2 * NDEF) * NDEF + inside % NDEF, -1
    )
    permute_columns(0, 3)
    finish_gather(0, 0)
    start_gather(0, 1)
    permute_columns(3, SAME // 256)
    start(column_exchange)
    finish_gather(0, 1)
    start_gather(0, 2)

    for copy in block_copies[:3]:
        copy.wait()
    precondition(field0, z0, field1, 0)
    for copy in block_copies[3:]:
        copy.wait()
    operate(field1, u0, 0, (1, L - 1), True)
    received(edge_exchange)
    padded_vectors[:NDEF, :W] = jnp.where(me > 0, edge_vectors[0], 0)
    padded_vectors[2 * NDEF:, (L + 1) * W:] = jnp.where(me < DEVICES - 1, edge_vectors[1], 0)

    @pl.loop(0, L)
    def _(plane):
        high, low = two_terms(banded(padded_vectors, coupling, plane))
        images[:3 * NDEF, lanes(plane)] = high
        images[128:128 + 3 * NDEF, lanes(plane)] = high
        images[256:256 + 3 * NDEF, lanes(plane)] = low
        own = padded_vectors[NDEF:2 * NDEF, lanes(plane + 1)]
        expansion[NDEF:2 * NDEF, lanes(plane)] = own
        expansion[128 + NDEF:128 + 2 * NDEF, lanes(plane)] = own

    vectors = padded_vectors[NDEF:2 * NDEF, W:(L + 1) * W]
    image_coupling[...] = dot(vectors, images[:128], NT) + dot(vectors, images[256:], NT)
    finish_halo(field1, 1)
    operate(field1, u0, 0, (0, 2), True)
    finish_gather(0, 2)
    received(column_exchange)
    finish_coarse(0)
    share_coefficients(
        projected[...] + dot(image_coupling[...], coarse[...], NN, lax.Precision.HIGHEST), 1
    )

    @pl.loop(0, 2)
    def _(i):
        add_image(u0, field2, edge(i), 0)

    start_halo(field2, 2)

    @pl.loop(1, L - 1)
    def _(plane):
        add_image(u0, field2, plane, 0)

    finish_gather(1, 0)
    start_gather(1, 1)
    inner_products(((0, v0, v0), (1, v0, u0), (2, u0, u0)))
    precondition(field2, z1, field3, 1)
    finish_gather(1, 1)
    start_gather(1, 2)
    operate(field3, u1, 1, (1, L - 1), False)
    finish_halo(field3, 3)
    operate(field3, u1, 1, (0, 2), False)
    add_expansion(z0, 0)
    finish_gather(1, 2)
    finish_coarse(1)

    @pl.loop(0, L)
    def _(plane):
        add_image(u1, None, plane, 1)

    inner_products(((3, v0, u1), (4, u0, u1), (5, u1, u1)))
    sums[...] = jnp.transpose(gram[...])[:8]

    pair = remote(sums, slots.at[0, 0], sum_send.at[0, 0], sum_recv.at[0, 0], core_id)
    pair.start()
    pair.wait()
    sums[...] = sums[...] + slots[0, 0]
    for stage, (spot, group) in enumerate(sum_groups):
        slots[1 + stage, spot] = sums[...]
        copies = [
            remote(
                slots.at[1 + stage, spot], slots.at[1 + stage, spot],
                sum_send.at[1 + stage, i], sum_recv.at[1 + stage, i], device,
            )
            for i, device in enumerate(group)
        ]
        for copy in copies:
            copy.start()
        if stage == 0:
            add_expansion(z1, 1)
        for copy in copies:
            copy.wait()
        sums[...] = (
            ((slots[1 + stage, 0] + slots[1 + stage, 1])
             + (slots[1 + stage, 2] + slots[1 + stage, 3]))
            + ((slots[1 + stage, 4] + slots[1 + stage, 5])
               + (slots[1 + stage, 6] + slots[1 + stage, 7]))
        )

    g00, g01, g11 = sums[0:1], sums[1:2], sums[2:3]
    g02, g12, g22 = sums[3:4], sums[4:5], sums[5:6]
    s0, s1, s2 = jnp.sqrt(g00), jnp.sqrt(g11), jnp.sqrt(g22)
    r01 = g01 / s0 / s1
    r02 = g02 / s0 / s2
    r11 = jnp.sqrt((1.0 - r01) * (1.0 + r01))
    r12 = (g12 / s1 / s2 - r01 * r02) / r11
    r22 = jnp.sqrt((1.0 - r02) * (1.0 + r02) - r12 * r12)
    n0 = r11 * r22
    n1 = r01 * r22
    n2 = r01 * r12 - r11 * r02
    share = n0 / (n0 * n0 + n1 * n1 + n2 * n2)
    relative_ref[...] = n0 * share
    scaled1 = -(share * n2) / r22
    weight1 = scaled1 * (s0 / s2) * IMAGE_SCALE
    weight0 = (share * n1 - scaled1 * r12) / r11 * (s0 / s1)
    gram[...] = jnp.transpose(
        jnp.concatenate([weight0, weight1, jnp.zeros((126, K), F32)], axis=0)
    )

    def solution_copy(plane):
        return pltpu.make_async_copy(z0.at[plane], solution_h.at[plane], out_sem.at[0, plane])

    def residual_copy(plane):
        return pltpu.make_async_copy(v0.at[plane], residual_h.at[plane], out_sem.at[1, plane])

    @pl.loop(0, L)
    def _(plane):
        first = gram[:, 0:1]
        second = gram[:, 1:2]
        z0[plane] = first * z0[plane] + second * z1[plane]
        solution_copy(plane).start()
        v0[plane] = v0[plane] - first * u0[plane] - second * u1[plane]
        residual_copy(plane).start()

    for copy in sends:
        copy.wait_send()

    @pl.loop(0, L)
    def _(plane):
        solution_copy(plane).wait()
        residual_copy(plane).wait()


def local(
    loads, diagonal_blocks, lower_coupling, upper_coupling, local_inverse, deflation,
    coarse_inverse, coarse_order,
):
    hbm = pl.BlockSpec(memory_space=pl.ANY)
    field = pltpu.VMEM((L, K, W), F32)
    padded = pltpu.VMEM((K, (L + 2) * W), BF16)
    blocks = pltpu.VMEM((L, 3, W, W), BF16)
    dma = pltpu.SemaphoreType.DMA
    answer, residual, relative = pl.pallas_call(
        kernel,
        out_shape=(
            jax.ShapeDtypeStruct((L, K, W), F32),
            jax.ShapeDtypeStruct((L, K, W), F32),
            jax.ShapeDtypeStruct((1, K), F32),
        ),
        in_specs=[hbm] * 8,
        out_specs=(hbm, hbm, pl.BlockSpec(memory_space=pltpu.VMEM)),
        scratch_shapes=[
            field, field, field, field, field,
            padded, padded, padded, padded,
            blocks, blocks,
            pltpu.VMEM((3 * NDEF, (L + 2) * W), BF16),
            pltpu.VMEM((2, NDEF, W), BF16),
            pltpu.VMEM((2 * 128, L * W), BF16),
            pltpu.VMEM((3 * 128, L * W), BF16),
            pltpu.VMEM((NDEF, 128), F32),
            pltpu.VMEM((NDEF, NCOARSE), F32),
            pltpu.VMEM((NDEF, NCOARSE), F32),
            pltpu.VMEM((4 * NDEF, NCOARSE), BF16),
            pltpu.VMEM((8 * NDEF, SAME), BF16),
            pltpu.VMEM((1, NCOARSE), jnp.int32),
            pltpu.VMEM((1, NCOARSE), jnp.int32),
            pltpu.VMEM((2, SIDE, SIDE, SIDE, NDEF, K), BF16),
            pltpu.VMEM((2, SIDE * NDEF, K), BF16),
            pltpu.VMEM((2, 4 * NDEF, K), F32),
            pltpu.VMEM((2, 3 * NDEF, K), F32),
            pltpu.VMEM((128, K), F32),
            pltpu.VMEM((2, K, 3 * 128), BF16),
            pltpu.VMEM((NDEF, K), F32),
            pltpu.VMEM((K, 128), F32),
            pltpu.VMEM((8, K), F32),
            pltpu.VMEM((3, 8, 8, K), F32),
            dma((L,)), dma((L,)), dma((6,)), dma((2,)), dma((2, L)),
            dma((4, 2)), dma((4, 2)), dma((2, 3, 3, 3)), dma((2, 3, 3, 3)),
            dma((1,)), dma((1,)), dma((2,)), dma((2,)), dma((4,)), dma((4,)),
            dma((2,)), dma((2,)), dma((3, 7)), dma((3, 7)),
        ],
        compiler_params=pltpu.CompilerParams(
            collective_id=0, has_side_effects=True, vmem_limit_bytes=60 * 2**20
        ),
        cost_estimate=pl.CostEstimate(
            flops=8 * 10**9, bytes_accessed=25 * 10**6, transcendentals=0
        ),
    )(
        loads, diagonal_blocks, lower_coupling, upper_coupling, local_inverse, deflation,
        coarse_inverse, coarse_order.reshape(1, NCOARSE),
    )
    return answer, residual, relative.reshape(K)


def solution(mesh):
    spread = P(("grp", "sub"))
    return jax.shard_map(
        local,
        mesh=mesh,
        in_specs=(
            spread, spread, spread, spread, P(None, ("grp", "sub")), spread, spread, P(),
        ),
        out_specs=(spread, spread, P()),
        check_vma=False,
    )
```

```python
import jax
import jax.numpy as jnp
from jax import lax
from jax.experimental import pallas as pl
from jax.experimental.pallas import tpu as pltpu
from jax.sharding import PartitionSpec as P

MESH = pl.DeviceIdType.MESH
F32 = jnp.float32
BF16 = jnp.bfloat16

L = 8
K = 256
W = 384
NDEF = 32
SIDE = 4
DEVICES = 128
SAME = SIDE * SIDE * SIDE * NDEF
NCOARSE = 2 * SAME
BAND = 3 * W
IMAGE_SCALE = 2.0 ** -24
INNER, OUTER = (1, L - 1), (0, 2)
GATHER_PARTS = (("xyz", 0, 16), ("zxy", 16, 32))
NN = (((1,), (0,)), ((), ()))
NT = (((1,), (1,)), ((), ()))


def lanes(plane):
    return pl.ds(pl.multiple_of(plane * W, W), W)


def dot(first, second, form=NN, precision=None):
    return lax.dot_general(
        first, second, form, precision=precision, preferred_element_type=F32
    )


def two_terms(value):
    high = value.astype(BF16)
    return high, (value - high.astype(F32)).astype(BF16)


def kernel(
    loads_h, diagonal_h, lower_h, upper_h, local_h, deflation_h, inverse_h, order_h,
    solution_h, residual_h, relative_ref,
    v0, z0, u0, z1, u1, field0, field1, field2, field3, precond, coupling,
    padded_vectors, edge_vectors, expansion, images, image_coupling,
    own_rows, other_rows, split_rows, columns, order, place, gathered, own_low,
    partial, other_partial, coarse, amounts, projected, gram, sums, slots,
    load_sem, vector_sem, block_sem, row_sem, out_sem,
    halo_send, halo_recv, gather_send, gather_recv, row_send, row_recv,
    edge_send, edge_recv, column_send, column_recv,
    partial_send, partial_recv, sum_send, sum_recv,
):
    grp = lax.axis_index("grp")
    sub = lax.axis_index("sub")
    y, z, x, core = grp // SIDE, grp % SIDE, sub // 2, sub % 2
    me = grp * 8 + sub
    place_of = {"x": x, "y": y, "z": z}

    def along_chain(step):
        device = (me + step + DEVICES) % DEVICES
        return (device // 8, device % 8)

    before_id, after_id = along_chain(-1), along_chain(1)
    chip_before_id, chip_after_id = along_chain(-2), along_chain(2)
    core_id = (grp, x * 2 + 1 - core)

    def chip(at_x, at_y, at_z):
        return (at_y * SIDE + at_z, at_x * 2 + core)

    def partner(axis, step):
        spot = dict(place_of)
        spot[axis] = (spot[axis] + step) % SIDE
        return chip(spot["x"], spot["y"], spot["z"])

    z_low, z_high = z % 2, z // 2
    sum_groups = (
        (z_low * SIDE + x, [
            chip((x + step) % SIDE, y, 2 * z_high + (z_low + flip) % 2)
            for flip in (0, 1) for step in range(SIDE) if flip or step
        ]),
        (z_high * SIDE + y, [
            chip(x, (y + step) % SIDE, 2 * ((z_high + flip) % 2) + z_low)
            for flip in (0, 1) for step in range(SIDE) if flip or step
        ]),
    )

    def load_copy(plane):
        return pltpu.make_async_copy(loads_h.at[plane], v0.at[plane], load_sem.at[plane])

    def vector_copy(plane):
        return pltpu.make_async_copy(
            deflation_h.at[plane], padded_vectors.at[NDEF:2 * NDEF, lanes(plane + 1)],
            vector_sem.at[plane],
        )

    block_copies = [
        pltpu.make_async_copy(source, target, block_sem.at[i])
        for i, (source, target) in enumerate([
            (local_h.at[0], precond.at[:, 0]),
            (local_h.at[1], precond.at[:, 1]),
            (local_h.at[2], precond.at[:, 2]),
            (lower_h, coupling.at[:, 0]),
            (diagonal_h, coupling.at[:, 1]),
            (upper_h, coupling.at[:, 2]),
        ])
    ]
    row_copy = pltpu.make_async_copy(inverse_h, own_rows, row_sem.at[0])
    order_copy = pltpu.make_async_copy(order_h, order, row_sem.at[1])
    for plane in (0, 7, 1, 2, 3, 4, 5, 6):
        load_copy(plane).start()
    for plane in range(L):
        vector_copy(plane).start()
    row_copy.start()
    order_copy.start()

    barrier = pltpu.get_barrier_semaphore()
    outer = (me + DEVICES - 1 + 2 * core) % DEVICES
    partners = [partner(axis, step) for axis in "xyz" for step in (1, 2, 3)]
    partners += [core_id, (outer // 8, outer % 8), chip_before_id, chip_after_id]
    for device in partners:
        pl.semaphore_signal(barrier, inc=1, device_id=device, device_id_type=MESH)

    padded_vectors[:NDEF] = jnp.zeros((NDEF, (L + 2) * W), BF16)
    padded_vectors[2 * NDEF:] = jnp.zeros((NDEF, (L + 2) * W), BF16)
    padded_vectors[NDEF:2 * NDEF, :W] = jnp.zeros((NDEF, W), BF16)
    padded_vectors[NDEF:2 * NDEF, (L + 1) * W:] = jnp.zeros((NDEF, W), BF16)
    expansion[...] = jnp.zeros((2 * 128, L * W), BF16)
    images[...] = jnp.zeros((3 * 128, L * W), BF16)
    own_low[...] = jnp.zeros((2, SIDE * NDEF, K), BF16)
    gram[...] = jnp.zeros((K, 128), F32)
    projected[...] = jnp.zeros((NDEF, K), F32)
    coarse[...] = jnp.zeros((128, K), F32)

    sends = []

    def remote(source, target, send, recv, device):
        return pltpu.make_async_remote_copy(
            src_ref=source, dst_ref=target, send_sem=send, recv_sem=recv,
            device_id=device, device_id_type=MESH,
        )

    def start(copies):
        for copy in copies:
            copy.start()
        sends.extend(copies)

    def received(copies):
        for copy in copies:
            copy.wait_recv()

    row_exchange = [
        remote(inverse_h, other_rows, row_send.at[0], row_recv.at[0], core_id)
    ]
    edge_exchange = [
        remote(
            deflation_h.at[0], edge_vectors.at[1], edge_send.at[0], edge_recv.at[0], before_id
        ),
        remote(
            deflation_h.at[L - 1], edge_vectors.at[0], edge_send.at[1], edge_recv.at[1], after_id
        ),
    ]
    column_exchange = [
        remote(
            columns.at[row:row + NDEF], columns.at[target:target + NDEF],
            column_send.at[i], column_recv.at[i], device,
        )
        for i, (row, target, device) in enumerate([
            (2 * NDEF, 0, chip_after_id),
            (6 * NDEF, 4 * NDEF, chip_after_id),
            (NDEF, 3 * NDEF, chip_before_id),
            (5 * NDEF, 7 * NDEF, chip_before_id),
        ])
    ]

    def halo_copies(field, which):
        return [
            remote(
                field.at[:, lanes(1)], field.at[:, lanes(L + 1)],
                halo_send.at[which, 0], halo_recv.at[which, 0], before_id,
            ),
            remote(
                field.at[:, lanes(L)], field.at[:, lanes(0)],
                halo_send.at[which, 1], halo_recv.at[which, 1], after_id,
            ),
        ]

    def start_halo(field, which):
        start(halo_copies(field, which))

    def finish_halo(field, which):
        received(halo_copies(field, which))

        @pl.when(me == 0)
        def _():
            field[:, lanes(0)] = jnp.zeros((K, W), BF16)

        @pl.when(me == DEVICES - 1)
        def _():
            field[:, lanes(L + 1)] = jnp.zeros((K, W), BF16)

    def gather_copies(which, stage):
        found = []
        for part, (axes, row0, row1) in enumerate(GATHER_PARTS):
            done = axes[:stage]
            spot = tuple(slice(None) if name in done else place_of[name] for name in "yzx")
            block = gathered.at[(which,) + spot + (slice(row0, row1),)]
            for step in (1, 2, 3):
                found.append(remote(
                    block, block,
                    gather_send.at[which, part, stage, step - 1],
                    gather_recv.at[which, part, stage, step - 1],
                    partner(axes[stage], step),
                ))
        return found

    def start_gather(which, stage):
        start(gather_copies(which, stage))

    def finish_gather(which, stage):
        received(gather_copies(which, stage))

    def share_coefficients(own, which):
        high, low = two_terms(own)
        gathered[which, y, z, x] = high
        start_gather(which, 0)
        own_low[which, pl.ds(pl.multiple_of(x * NDEF, NDEF), NDEF)] = low

    def banded(field, blocks, plane):
        window = field[:, pl.ds(pl.multiple_of(plane * W, W), BAND)]
        return dot(window, blocks[plane].reshape(BAND, W))

    def edge(i):
        return i * (L - 1)

    def finish_coarse(which):
        product = dot(columns[...], gathered[which].reshape(SAME, K))
        window = pl.ds(pl.multiple_of((y * SIDE + z) * 128, 128), 128)
        fix = dot(columns[:4 * NDEF, window], own_low[which])
        partial[which] = product[:4 * NDEF] + (product[4 * NDEF:] + fix)
        exchange = [remote(
            partial.at[which, pl.ds(pl.multiple_of((1 - core) * NDEF, NDEF), 3 * NDEF)],
            other_partial.at[which], partial_send.at[which], partial_recv.at[which], core_id,
        )]
        start(exchange)
        received(exchange)
        coarse[:3 * NDEF] = (
            partial[which, pl.ds(pl.multiple_of(core * NDEF, NDEF), 3 * NDEF)]
            + other_partial[which]
        )
        high, low = two_terms(jnp.transpose(coarse[...]))
        amounts[which, :, :128] = high
        amounts[which, :, 128:256] = low
        amounts[which, :, 256:] = high

    def precondition(field, result, rounded, planes):
        @pl.loop(*planes)
        def _(i):
            plane = i if planes == INNER else edge(i)
            value = banded(field, precond, plane)
            result[plane] = value
            rounded[:, lanes(plane + 1)] = value.astype(BF16)

    def operate(field, result, planes, project):
        @pl.loop(*planes)
        def _(i):
            plane = i if planes == INNER else edge(i)
            image = banded(field, coupling, plane)
            result[plane] = image
            if project:
                projected[...] += dot(
                    padded_vectors[NDEF:2 * NDEF, lanes(plane + 1)], image.astype(BF16), NT
                )

    def add_image(result, rounded, plane, which):
        total = result[plane] + dot(amounts[which], images[:, lanes(plane)])
        result[plane] = total
        if rounded is not None:
            rounded[:, lanes(plane + 1)] = total.astype(BF16)

    def add_expansion(result, which):
        @pl.loop(0, L)
        def _(plane):
            result[plane] += dot(amounts[which, :, :256], expansion[:, lanes(plane)])

    def inner_products(fields, pairs):
        rows = 32

        @pl.loop(0, K // rows)
        def _(chunk):
            span = pl.ds(pl.multiple_of(chunk * rows, rows), rows)
            totals = [jnp.zeros((rows, 128), F32) for _ in pairs]
            for plane in range(L):
                for lane in range(0, W, 128):
                    values = [field[plane, span, lane:lane + 128] for field in fields]
                    if len(values) == 3:
                        values[2] = values[2] * IMAGE_SCALE
                    totals = [
                        total + values[first] * values[second]
                        for total, (_, first, second) in zip(totals, pairs)
                    ]
            for total, (column, _, _) in zip(totals, pairs):
                gram[span, column:column + 1] = jnp.sum(total, axis=1, keepdims=True)

    def permute_columns(first, last):
        @pl.loop(first, last)
        def _(block):
            base = block * 256
            total = jnp.zeros((4 * NDEF, 256), F32)
            for part in range(4):
                span = slice(part * 1024, (part + 1) * 1024)
                row = lax.broadcasted_iota(jnp.int32, (256, 1024), 0)
                hot = jnp.where(place[:, span] - base == row, 1.0, 0.0).astype(BF16)
                total += dot(split_rows[:, span], hot, NT)
            target = pl.ds(pl.multiple_of(base, 256), 256)
            columns[NDEF:3 * NDEF, target] = total[:2 * NDEF].astype(BF16)
            columns[5 * NDEF:7 * NDEF, target] = total[2 * NDEF:].astype(BF16)

    for plane in (0, 7, 1, 2, 3, 4, 5, 6):
        load_copy(plane).wait()
        field0[:, lanes(plane + 1)] = v0[plane].astype(BF16)

    for plane in range(L):
        vector_copy(plane).wait()
    for copy in block_copies:
        copy.start()
    first_coefficients = dot(
        padded_vectors[NDEF:2 * NDEF, W:(L + 1) * W], field0[:, W:(L + 1) * W], NT
    )
    pl.semaphore_wait(barrier, len(partners))
    share_coefficients(first_coefficients, 0)
    start(row_exchange)
    start_halo(field0, 0)
    start(edge_exchange)

    row_copy.wait()
    order_copy.wait()
    received(row_exchange)
    for rows, owner in ((own_rows, core), (other_rows, 1 - core)):
        high, low = two_terms(rows[...])
        split_rows[pl.ds(pl.multiple_of(owner * NDEF, NDEF), NDEF)] = high
        split_rows[pl.ds(pl.multiple_of((2 + owner) * NDEF, NDEF), NDEF)] = low
    unknown = order[...]
    inside = unknown % (2 * NDEF)
    place[...] = jnp.where(
        inside // NDEF == core, unknown // (2 * NDEF) * NDEF + inside % NDEF, -1
    )
    permute_columns(0, 3)
    finish_gather(0, 0)
    start_gather(0, 1)
    permute_columns(3, SAME // 256)
    start(column_exchange)
    finish_gather(0, 1)
    start_gather(0, 2)

    for copy in block_copies[:3]:
        copy.wait()
    finish_halo(field0, 0)
    precondition(field0, z0, field1, OUTER)
    start_halo(field1, 1)
    precondition(field0, z0, field1, INNER)
    for copy in block_copies[3:]:
        copy.wait()
    operate(field1, u0, INNER, True)
    received(edge_exchange)
    padded_vectors[:NDEF, :W] = jnp.where(me > 0, edge_vectors[0], 0)
    padded_vectors[2 * NDEF:, (L + 1) * W:] = jnp.where(me < DEVICES - 1, edge_vectors[1], 0)

    @pl.loop(0, L)
    def _(plane):
        high, low = two_terms(banded(padded_vectors, coupling, plane))
        images[:3 * NDEF, lanes(plane)] = high
        images[128:128 + 3 * NDEF, lanes(plane)] = high
        images[256:256 + 3 * NDEF, lanes(plane)] = low
        own = padded_vectors[NDEF:2 * NDEF, lanes(plane + 1)]
        expansion[NDEF:2 * NDEF, lanes(plane)] = own
        expansion[128 + NDEF:128 + 2 * NDEF, lanes(plane)] = own

    vectors = padded_vectors[NDEF:2 * NDEF, W:(L + 1) * W]
    image_coupling[...] = dot(vectors, images[:128], NT) + dot(vectors, images[256:], NT)
    finish_halo(field1, 1)
    operate(field1, u0, OUTER, True)
    finish_gather(0, 2)
    received(column_exchange)
    finish_coarse(0)
    share_coefficients(
        projected[...] + dot(image_coupling[...], coarse[...], NN, lax.Precision.HIGHEST), 1
    )

    @pl.loop(0, 2)
    def _(i):
        add_image(u0, field2, edge(i), 0)

    start_halo(field2, 2)

    @pl.loop(1, L - 1)
    def _(plane):
        add_image(u0, field2, plane, 0)

    finish_gather(1, 0)
    start_gather(1, 1)
    inner_products((v0, u0), ((0, 0, 0), (1, 0, 1), (2, 1, 1)))
    precondition(field2, z1, field3, INNER)
    finish_gather(1, 1)
    start_gather(1, 2)
    finish_halo(field2, 2)
    precondition(field2, z1, field3, OUTER)
    start_halo(field3, 3)
    operate(field3, u1, INNER, False)
    add_expansion(z0, 0)
    finish_halo(field3, 3)
    operate(field3, u1, OUTER, False)
    finish_gather(1, 2)
    finish_coarse(1)

    @pl.loop(0, L)
    def _(plane):
        add_image(u1, None, plane, 1)

    inner_products((v0, u0, u1), ((3, 0, 2), (4, 1, 2), (5, 2, 2)))
    sums[...] = jnp.transpose(gram[...])[:8]

    pair = remote(sums, slots.at[0, 0], sum_send.at[0, 0], sum_recv.at[0, 0], core_id)
    pair.start()
    pair.wait()
    sums[...] = sums[...] + slots[0, 0]
    for stage, (spot, group) in enumerate(sum_groups):
        slots[1 + stage, spot] = sums[...]
        copies = [
            remote(
                slots.at[1 + stage, spot], slots.at[1 + stage, spot],
                sum_send.at[1 + stage, i], sum_recv.at[1 + stage, i], device,
            )
            for i, device in enumerate(group)
        ]
        for copy in copies:
            copy.start()
        if stage == 0:
            add_expansion(z1, 1)
        for copy in copies:
            copy.wait()
        sums[...] = (
            ((slots[1 + stage, 0] + slots[1 + stage, 1])
             + (slots[1 + stage, 2] + slots[1 + stage, 3]))
            + ((slots[1 + stage, 4] + slots[1 + stage, 5])
               + (slots[1 + stage, 6] + slots[1 + stage, 7]))
        )

    g00, g01, g11 = sums[0:1], sums[1:2], sums[2:3]
    g02, g12, g22 = sums[3:4], sums[4:5], sums[5:6]
    s0, s1, s2 = jnp.sqrt(g00), jnp.sqrt(g11), jnp.sqrt(g22)
    r01 = g01 / s0 / s1
    r02 = g02 / s0 / s2
    r11 = jnp.sqrt((1.0 - r01) * (1.0 + r01))
    r12 = (g12 / s1 / s2 - r01 * r02) / r11
    r22 = jnp.sqrt((1.0 - r02) * (1.0 + r02) - r12 * r12)
    n0 = r11 * r22
    n1 = r01 * r22
    n2 = r01 * r12 - r11 * r02
    share = n0 / (n0 * n0 + n1 * n1 + n2 * n2)
    relative_ref[...] = n0 * share
    scaled1 = -(share * n2) / r22
    weight1 = scaled1 * (s0 / s2) * IMAGE_SCALE
    weight0 = (share * n1 - scaled1 * r12) / r11 * (s0 / s1)
    gram[...] = jnp.transpose(
        jnp.concatenate([weight0, weight1, jnp.zeros((126, K), F32)], axis=0)
    )

    def solution_copy(plane):
        return pltpu.make_async_copy(z0.at[plane], solution_h.at[plane], out_sem.at[0, plane])

    def residual_copy(plane):
        return pltpu.make_async_copy(v0.at[plane], residual_h.at[plane], out_sem.at[1, plane])

    @pl.loop(0, L)
    def _(plane):
        first, second = gram[:, 0:1], gram[:, 1:2]
        z0[plane] = first * z0[plane] + second * z1[plane]
        solution_copy(plane).start()
        v0[plane] = v0[plane] - first * u0[plane] - second * u1[plane]
        residual_copy(plane).start()

    for copy in sends:
        copy.wait_send()

    @pl.loop(0, L)
    def _(plane):
        solution_copy(plane).wait()
        residual_copy(plane).wait()


def deliver(
    answer, residual, relative, answer_out, residual_out, relative_out, held, held_row, sems
):
    def through(source, between, target, i, j):
        return (
            pltpu.make_async_copy(source, between, sems.at[0, i, j]),
            pltpu.make_async_copy(between, target, sems.at[1, i, j]),
        )

    steps = [
        through(source.at[plane], held.at[i, plane], target.at[plane], i, plane)
        for plane in range(L)
        for i, (source, target) in enumerate(((answer, answer_out), (residual, residual_out)))
    ]
    steps.append(through(relative, held_row, relative_out, 2, 0))
    for fetch, _ in steps:
        fetch.start()
    for fetch, store in steps:
        fetch.wait()
        store.start()
    for _, store in steps:
        store.wait()


def local(
    loads, diagonal_blocks, lower_coupling, upper_coupling, local_inverse, deflation,
    coarse_inverse, coarse_order,
):
    hbm = pl.BlockSpec(memory_space=pl.ANY)
    field = pltpu.VMEM((L, K, W), F32)
    padded = pltpu.VMEM((K, (L + 2) * W), BF16)
    blocks = pltpu.VMEM((L, 3, W, W), BF16)
    dma = pltpu.SemaphoreType.DMA
    fields = jax.ShapeDtypeStruct((L, K, W), F32)
    outs = (fields, fields, jax.ShapeDtypeStruct((1, K), F32))
    results = pl.pallas_call(
        kernel,
        out_shape=outs,
        in_specs=[hbm] * 8,
        out_specs=(hbm, hbm, pl.BlockSpec(memory_space=pltpu.VMEM)),
        scratch_shapes=[
            field, field, field, field, field,
            padded, padded, padded, padded,
            blocks, blocks,
            pltpu.VMEM((3 * NDEF, (L + 2) * W), BF16),
            pltpu.VMEM((2, NDEF, W), BF16),
            pltpu.VMEM((2 * 128, L * W), BF16),
            pltpu.VMEM((3 * 128, L * W), BF16),
            pltpu.VMEM((NDEF, 128), F32),
            pltpu.VMEM((NDEF, NCOARSE), F32),
            pltpu.VMEM((NDEF, NCOARSE), F32),
            pltpu.VMEM((4 * NDEF, NCOARSE), BF16),
            pltpu.VMEM((8 * NDEF, SAME), BF16),
            pltpu.VMEM((1, NCOARSE), jnp.int32),
            pltpu.VMEM((1, NCOARSE), jnp.int32),
            pltpu.VMEM((2, SIDE, SIDE, SIDE, NDEF, K), BF16),
            pltpu.VMEM((2, SIDE * NDEF, K), BF16),
            pltpu.VMEM((2, 4 * NDEF, K), F32),
            pltpu.VMEM((2, 3 * NDEF, K), F32),
            pltpu.VMEM((128, K), F32),
            pltpu.VMEM((2, K, 3 * 128), BF16),
            pltpu.VMEM((NDEF, K), F32),
            pltpu.VMEM((K, 128), F32),
            pltpu.VMEM((8, K), F32),
            pltpu.VMEM((3, 8, 8, K), F32),
            dma((L,)), dma((L,)), dma((6,)), dma((2,)), dma((2, L)),
            dma((4, 2)), dma((4, 2)), dma((2, 2, 3, 3)), dma((2, 2, 3, 3)),
            dma((1,)), dma((1,)), dma((2,)), dma((2,)), dma((4,)), dma((4,)),
            dma((2,)), dma((2,)), dma((3, 7)), dma((3, 7)),
        ],
        compiler_params=pltpu.CompilerParams(
            collective_id=0, has_side_effects=True, vmem_limit_bytes=60 * 2**20
        ),
        cost_estimate=pl.CostEstimate(
            flops=8 * 10**9, bytes_accessed=25 * 10**6, transcendentals=0
        ),
    )(
        loads, diagonal_blocks, lower_coupling, upper_coupling, local_inverse, deflation,
        coarse_inverse, coarse_order.reshape(1, NCOARSE),
    )
    answer, residual, ratio = pl.pallas_call(
        deliver,
        out_shape=outs,
        in_specs=[hbm] * 3,
        out_specs=(hbm,) * 3,
        scratch_shapes=[pltpu.VMEM((2, L, K, W), F32), pltpu.VMEM((1, K), F32), dma((2, 3, L))],
        compiler_params=pltpu.CompilerParams(vmem_limit_bytes=60 * 2**20),
    )(*results)
    return answer, residual, ratio.reshape(K)


def solution(mesh):
    spread = P(("grp", "sub"))
    return jax.shard_map(
        local,
        mesh=mesh,
        in_specs=(
            spread, spread, spread, spread, P(None, ("grp", "sub")), spread, spread, P(),
        ),
        out_specs=(spread, spread, P()),
        check_vma=False,
    )
```

```python
import jax
import jax.numpy as jnp
from jax import lax
from jax.experimental import pallas as pl
from jax.experimental.pallas import tpu as pltpu
from jax.sharding import PartitionSpec as P

MESH = pl.DeviceIdType.MESH
F32 = jnp.float32
BF16 = jnp.bfloat16

L = 8
K = 256
W = 384
NDEF = 32
SIDE = 4
DEVICES = 128
SAME = SIDE * SIDE * SIDE * NDEF
NCOARSE = 2 * SAME
BAND = 3 * W
IMAGE_SCALE = 2.0 ** -24
INNER, OUTER = (1, L - 1), (0, 2)
GATHER_PARTS = (("xyz", 0, 16), ("zxy", 16, 32))
NN = (((1,), (0,)), ((), ()))
NT = (((1,), (1,)), ((), ()))


def lanes(plane):
    return pl.ds(pl.multiple_of(plane * W, W), W)


def dot(first, second, form=NN, precision=None):
    return lax.dot_general(
        first, second, form, precision=precision, preferred_element_type=F32
    )


def two_terms(value):
    high = value.astype(BF16)
    return high, (value - high.astype(F32)).astype(BF16)


def kernel(
    loads_h, diagonal_h, lower_h, upper_h, local_h, deflation_h, inverse_h, order_h,
    solution_h, residual_h, relative_ref,
    v0, z0, u0, z1, u1, field0, field1, field2, field3, precond, coupling,
    padded_vectors, edge_vectors, expansion, images, image_coupling,
    own_rows, other_rows, split_rows, columns, order, place, gathered, own_low,
    partial, other_partial, coarse, amounts, projected, gram, sums, slots,
    load_sem, vector_sem, block_sem, row_sem, out_sem,
    halo_send, halo_recv, gather_send, gather_recv, row_send, row_recv,
    edge_send, edge_recv, column_send, column_recv,
    partial_send, partial_recv, sum_send, sum_recv,
):
    grp = lax.axis_index("grp")
    sub = lax.axis_index("sub")
    y, z, x, core = grp // SIDE, grp % SIDE, sub // 2, sub % 2
    me = grp * 8 + sub
    place_of = {"x": x, "y": y, "z": z}

    def along_chain(step):
        device = (me + step + DEVICES) % DEVICES
        return (device // 8, device % 8)

    before_id, after_id = along_chain(-1), along_chain(1)
    chip_before_id, chip_after_id = along_chain(-2), along_chain(2)
    core_id = (grp, x * 2 + 1 - core)

    def chip(at_x, at_y, at_z):
        return (at_y * SIDE + at_z, at_x * 2 + core)

    def partner(axis, step):
        spot = dict(place_of)
        spot[axis] = (spot[axis] + step) % SIDE
        return chip(spot["x"], spot["y"], spot["z"])

    z_low, z_high = z % 2, z // 2
    sum_groups = (
        (z_low * SIDE + x, [
            chip((x + step) % SIDE, y, 2 * z_high + (z_low + flip) % 2)
            for flip in (0, 1) for step in range(SIDE) if flip or step
        ]),
        (z_high * SIDE + y, [
            chip(x, (y + step) % SIDE, 2 * ((z_high + flip) % 2) + z_low)
            for flip in (0, 1) for step in range(SIDE) if flip or step
        ]),
    )

    def load_copy(plane):
        return pltpu.make_async_copy(loads_h.at[plane], v0.at[plane], load_sem.at[plane])

    def vector_copy(plane):
        return pltpu.make_async_copy(
            deflation_h.at[plane], padded_vectors.at[NDEF:2 * NDEF, lanes(plane + 1)],
            vector_sem.at[plane],
        )

    block_copies = [
        pltpu.make_async_copy(source, target, block_sem.at[i])
        for i, (source, target) in enumerate([
            (local_h.at[0], precond.at[:, 0]),
            (local_h.at[1], precond.at[:, 1]),
            (local_h.at[2], precond.at[:, 2]),
            (lower_h, coupling.at[:, 0]),
            (diagonal_h, coupling.at[:, 1]),
            (upper_h, coupling.at[:, 2]),
        ])
    ]
    row_copy = pltpu.make_async_copy(inverse_h, own_rows, row_sem.at[0])
    order_copy = pltpu.make_async_copy(order_h, order, row_sem.at[1])
    for plane in (0, 7, 1, 2, 3, 4, 5, 6):
        load_copy(plane).start()
    for plane in range(L):
        vector_copy(plane).start()
    row_copy.start()
    order_copy.start()

    barrier = pltpu.get_barrier_semaphore()
    outer = (me + DEVICES - 1 + 2 * core) % DEVICES
    partners = [partner(axis, step) for axis in "xyz" for step in (1, 2, 3)]
    partners += [core_id, (outer // 8, outer % 8), chip_before_id, chip_after_id]
    for device in partners:
        pl.semaphore_signal(barrier, inc=1, device_id=device, device_id_type=MESH)

    padded_vectors[:NDEF] = jnp.zeros((NDEF, (L + 2) * W), BF16)
    padded_vectors[2 * NDEF:] = jnp.zeros((NDEF, (L + 2) * W), BF16)
    padded_vectors[NDEF:2 * NDEF, :W] = jnp.zeros((NDEF, W), BF16)
    padded_vectors[NDEF:2 * NDEF, (L + 1) * W:] = jnp.zeros((NDEF, W), BF16)
    expansion[...] = jnp.zeros((2 * 128, L * W), BF16)
    images[...] = jnp.zeros((3 * 128, L * W), BF16)
    columns[4 * NDEF:5 * NDEF] = jnp.zeros((NDEF, SAME), BF16)
    columns[7 * NDEF:] = jnp.zeros((NDEF, SAME), BF16)
    own_low[...] = jnp.zeros((2, SIDE * NDEF, K), BF16)
    gram[...] = jnp.zeros((K, 128), F32)
    projected[...] = jnp.zeros((NDEF, K), F32)
    coarse[...] = jnp.zeros((128, K), F32)

    sends = []

    def remote(source, target, send, recv, device):
        return pltpu.make_async_remote_copy(
            src_ref=source, dst_ref=target, send_sem=send, recv_sem=recv,
            device_id=device, device_id_type=MESH,
        )

    def start(copies):
        for copy in copies:
            copy.start()
        sends.extend(copies)

    def received(copies):
        for copy in copies:
            copy.wait_recv()

    row_exchange = [
        remote(inverse_h, other_rows, row_send.at[0], row_recv.at[0], core_id)
    ]
    edge_exchange = [
        remote(
            deflation_h.at[0], edge_vectors.at[1], edge_send.at[0], edge_recv.at[0], before_id
        ),
        remote(
            deflation_h.at[L - 1], edge_vectors.at[0], edge_send.at[1], edge_recv.at[1], after_id
        ),
    ]
    column_exchange = [
        remote(
            columns.at[row:row + NDEF], columns.at[target:target + NDEF],
            column_send.at[i], column_recv.at[i], device,
        )
        for i, (row, target, device) in enumerate([
            (2 * NDEF, 0, chip_after_id),
            (NDEF, 3 * NDEF, chip_before_id),
        ])
    ]

    def halo_copies(field, which):
        return [
            remote(
                field.at[:, lanes(1)], field.at[:, lanes(L + 1)],
                halo_send.at[which, 0], halo_recv.at[which, 0], before_id,
            ),
            remote(
                field.at[:, lanes(L)], field.at[:, lanes(0)],
                halo_send.at[which, 1], halo_recv.at[which, 1], after_id,
            ),
        ]

    def start_halo(field, which):
        start(halo_copies(field, which))

    def finish_halo(field, which):
        received(halo_copies(field, which))

        @pl.when(me == 0)
        def _():
            field[:, lanes(0)] = jnp.zeros((K, W), BF16)

        @pl.when(me == DEVICES - 1)
        def _():
            field[:, lanes(L + 1)] = jnp.zeros((K, W), BF16)

    def gather_copies(which, stage):
        found = []
        for part, (axes, row0, row1) in enumerate(GATHER_PARTS):
            done = axes[:stage]
            spot = tuple(slice(None) if name in done else place_of[name] for name in "yzx")
            block = gathered.at[(which,) + spot + (slice(row0, row1),)]
            for step in (1, 2, 3):
                found.append(remote(
                    block, block,
                    gather_send.at[which, part, stage, step - 1],
                    gather_recv.at[which, part, stage, step - 1],
                    partner(axes[stage], step),
                ))
        return found

    def start_gather(which, stage):
        start(gather_copies(which, stage))

    def finish_gather(which, stage):
        received(gather_copies(which, stage))

    def share_coefficients(own, which):
        high, low = two_terms(own)
        gathered[which, y, z, x] = high
        start_gather(which, 0)
        own_low[which, pl.ds(pl.multiple_of(x * NDEF, NDEF), NDEF)] = low

    def banded(field, blocks, plane):
        window = field[:, pl.ds(pl.multiple_of(plane * W, W), BAND)]
        return dot(window, blocks[plane].reshape(BAND, W))

    def edge(i):
        return i * (L - 1)

    def finish_coarse(which):
        product = dot(columns[...], gathered[which].reshape(SAME, K))
        window = pl.ds(pl.multiple_of((y * SIDE + z) * 128, 128), 128)
        fix = dot(columns[:4 * NDEF, window], own_low[which])
        partial[which] = product[:4 * NDEF] + (product[4 * NDEF:] + fix)
        exchange = [remote(
            partial.at[which, pl.ds(pl.multiple_of((1 - core) * NDEF, NDEF), 3 * NDEF)],
            other_partial.at[which], partial_send.at[which], partial_recv.at[which], core_id,
        )]
        start(exchange)
        received(exchange)
        coarse[:3 * NDEF] = (
            partial[which, pl.ds(pl.multiple_of(core * NDEF, NDEF), 3 * NDEF)]
            + other_partial[which]
        )
        high, low = two_terms(jnp.transpose(coarse[...]))
        amounts[which, :, :128] = high
        amounts[which, :, 128:256] = low
        amounts[which, :, 256:] = high

    def precondition(field, result, rounded, planes):
        @pl.loop(*planes)
        def _(i):
            plane = i if planes == INNER else edge(i)
            value = banded(field, precond, plane)
            result[plane] = value
            rounded[:, lanes(plane + 1)] = value.astype(BF16)

    def operate(field, result, planes, project):
        @pl.loop(*planes)
        def _(i):
            plane = i if planes == INNER else edge(i)
            image = banded(field, coupling, plane)
            result[plane] = image
            if project:
                projected[...] += dot(
                    padded_vectors[NDEF:2 * NDEF, lanes(plane + 1)], image.astype(BF16), NT
                )

    def add_image(result, rounded, plane, which):
        total = result[plane] + dot(amounts[which], images[:, lanes(plane)])
        result[plane] = total
        if rounded is not None:
            rounded[:, lanes(plane + 1)] = total.astype(BF16)

    def add_expansion(result, which):
        @pl.loop(0, L)
        def _(plane):
            result[plane] += dot(amounts[which, :, :256], expansion[:, lanes(plane)])

    def inner_products(fields, pairs):
        rows = 32

        @pl.loop(0, K // rows)
        def _(chunk):
            span = pl.ds(pl.multiple_of(chunk * rows, rows), rows)
            totals = [jnp.zeros((rows, 128), F32) for _ in pairs]
            for plane in range(L):
                for lane in range(0, W, 128):
                    values = [field[plane, span, lane:lane + 128] for field in fields]
                    if len(values) == 3:
                        values[2] = values[2] * IMAGE_SCALE
                    totals = [
                        total + values[first] * values[second]
                        for total, (_, first, second) in zip(totals, pairs)
                    ]
            for total, (column, _, _) in zip(totals, pairs):
                gram[span, column:column + 1] = jnp.sum(total, axis=1, keepdims=True)

    def permute_columns(first, last):
        @pl.loop(first, last)
        def _(block):
            base = block * 256
            total = jnp.zeros((256, 4 * NDEF), F32)
            for part in range(4):
                span = slice(part * 1024, (part + 1) * 1024)
                spot = place[:, span] - base
                inside = (spot >= 0) & (spot < 256)
                spot = jnp.where(inside, spot, -1).astype(F32).astype(BF16)
                row = lax.broadcasted_iota(jnp.int32, (256, 1024), 0).astype(F32).astype(BF16)
                hot = jnp.where(spot == row, jnp.ones((), BF16), jnp.zeros((), BF16))
                total += dot(hot, split_rows[:, span], NT)
            total = jnp.transpose(total).astype(BF16)
            target = pl.ds(pl.multiple_of(base, 256), 256)
            columns[NDEF:3 * NDEF, target] = total[:2 * NDEF]
            columns[5 * NDEF:7 * NDEF, target] = total[2 * NDEF:]

    for plane in (0, 7, 1, 2, 3, 4, 5, 6):
        load_copy(plane).wait()
        field0[:, lanes(plane + 1)] = v0[plane].astype(BF16)

    for plane in range(L):
        vector_copy(plane).wait()
    for copy in block_copies:
        copy.start()
    first_coefficients = dot(
        padded_vectors[NDEF:2 * NDEF, W:(L + 1) * W], field0[:, W:(L + 1) * W], NT
    )
    pl.semaphore_wait(barrier, len(partners))
    share_coefficients(first_coefficients, 0)
    start(row_exchange)
    start_halo(field0, 0)
    start(edge_exchange)

    row_copy.wait()
    order_copy.wait()
    received(row_exchange)
    for rows, owner in ((own_rows, core), (other_rows, 1 - core)):
        high, low = two_terms(rows[...])
        split_rows[pl.ds(pl.multiple_of(owner * NDEF, NDEF), NDEF)] = high
        split_rows[pl.ds(pl.multiple_of((2 + owner) * NDEF, NDEF), NDEF)] = low
    unknown = order[...]
    inside = unknown % (2 * NDEF)
    place[...] = jnp.where(
        inside // NDEF == core, unknown // (2 * NDEF) * NDEF + inside % NDEF, -1
    )
    permute_columns(0, 4)
    finish_gather(0, 0)
    start_gather(0, 1)
    permute_columns(4, SAME // 256)
    finish_gather(0, 1)
    start_gather(0, 2)
    start(column_exchange)

    for copy in block_copies[:3]:
        copy.wait()
    finish_halo(field0, 0)
    precondition(field0, z0, field1, OUTER)
    start_halo(field1, 1)
    precondition(field0, z0, field1, INNER)
    for copy in block_copies[3:]:
        copy.wait()
    operate(field1, u0, INNER, True)
    received(edge_exchange)
    padded_vectors[:NDEF, :W] = jnp.where(me > 0, edge_vectors[0], 0)
    padded_vectors[2 * NDEF:, (L + 1) * W:] = jnp.where(me < DEVICES - 1, edge_vectors[1], 0)

    @pl.loop(0, L)
    def _(plane):
        high, low = two_terms(banded(padded_vectors, coupling, plane))
        images[:3 * NDEF, lanes(plane)] = high
        images[128:128 + 3 * NDEF, lanes(plane)] = high
        images[256:256 + 3 * NDEF, lanes(plane)] = low
        own = padded_vectors[NDEF:2 * NDEF, lanes(plane + 1)]
        expansion[NDEF:2 * NDEF, lanes(plane)] = own
        expansion[128 + NDEF:128 + 2 * NDEF, lanes(plane)] = own

    vectors = padded_vectors[NDEF:2 * NDEF, W:(L + 1) * W]
    image_coupling[...] = dot(vectors, images[:128], NT) + dot(vectors, images[256:], NT)
    finish_halo(field1, 1)
    operate(field1, u0, OUTER, True)
    finish_gather(0, 2)
    received(column_exchange)
    finish_coarse(0)
    share_coefficients(
        projected[...] + dot(image_coupling[...], coarse[...], NN, lax.Precision.HIGHEST), 1
    )

    @pl.loop(0, 2)
    def _(i):
        add_image(u0, field2, edge(i), 0)

    start_halo(field2, 2)

    @pl.loop(1, L - 1)
    def _(plane):
        add_image(u0, field2, plane, 0)

    finish_gather(1, 0)
    start_gather(1, 1)
    inner_products((v0, u0), ((0, 0, 0), (1, 0, 1), (2, 1, 1)))
    precondition(field2, z1, field3, INNER)
    finish_gather(1, 1)
    start_gather(1, 2)
    finish_halo(field2, 2)
    precondition(field2, z1, field3, OUTER)
    start_halo(field3, 3)
    operate(field3, u1, INNER, False)
    add_expansion(z0, 0)
    finish_halo(field3, 3)
    operate(field3, u1, OUTER, False)
    finish_gather(1, 2)
    finish_coarse(1)

    @pl.loop(0, L)
    def _(plane):
        add_image(u1, None, plane, 1)

    inner_products((v0, u0, u1), ((3, 0, 2), (4, 1, 2), (5, 2, 2)))
    sums[...] = jnp.transpose(gram[...])[:8]

    pair = remote(sums, slots.at[0, 0], sum_send.at[0, 0], sum_recv.at[0, 0], core_id)
    pair.start()
    pair.wait()
    sums[...] = sums[...] + slots[0, 0]
    for stage, (spot, group) in enumerate(sum_groups):
        slots[1 + stage, spot] = sums[...]
        copies = [
            remote(
                slots.at[1 + stage, spot], slots.at[1 + stage, spot],
                sum_send.at[1 + stage, i], sum_recv.at[1 + stage, i], device,
            )
            for i, device in enumerate(group)
        ]
        for copy in copies:
            copy.start()
        if stage == 0:
            add_expansion(z1, 1)
        for copy in copies:
            copy.wait()
        sums[...] = (
            ((slots[1 + stage, 0] + slots[1 + stage, 1])
             + (slots[1 + stage, 2] + slots[1 + stage, 3]))
            + ((slots[1 + stage, 4] + slots[1 + stage, 5])
               + (slots[1 + stage, 6] + slots[1 + stage, 7]))
        )

    g00, g01, g11 = sums[0:1], sums[1:2], sums[2:3]
    g02, g12, g22 = sums[3:4], sums[4:5], sums[5:6]
    s0, s1, s2 = jnp.sqrt(g00), jnp.sqrt(g11), jnp.sqrt(g22)
    r01 = g01 / s0 / s1
    r02 = g02 / s0 / s2
    r11 = jnp.sqrt((1.0 - r01) * (1.0 + r01))
    r12 = (g12 / s1 / s2 - r01 * r02) / r11
    r22 = jnp.sqrt((1.0 - r02) * (1.0 + r02) - r12 * r12)
    n0 = r11 * r22
    n1 = r01 * r22
    n2 = r01 * r12 - r11 * r02
    share = n0 / (n0 * n0 + n1 * n1 + n2 * n2)
    relative_ref[...] = n0 * share
    scaled1 = -(share * n2) / r22
    weight1 = scaled1 * (s0 / s2) * IMAGE_SCALE
    weight0 = (share * n1 - scaled1 * r12) / r11 * (s0 / s1)
    gram[...] = jnp.transpose(
        jnp.concatenate([weight0, weight1, jnp.zeros((126, K), F32)], axis=0)
    )

    def solution_copy(plane):
        return pltpu.make_async_copy(z0.at[plane], solution_h.at[plane], out_sem.at[0, plane])

    def residual_copy(plane):
        return pltpu.make_async_copy(v0.at[plane], residual_h.at[plane], out_sem.at[1, plane])

    @pl.loop(0, L)
    def _(plane):
        first, second = gram[:, 0:1], gram[:, 1:2]
        z0[plane] = first * z0[plane] + second * z1[plane]
        solution_copy(plane).start()
        v0[plane] = v0[plane] - first * u0[plane] - second * u1[plane]
        residual_copy(plane).start()

    for copy in sends:
        copy.wait_send()

    @pl.loop(0, L)
    def _(plane):
        solution_copy(plane).wait()
        residual_copy(plane).wait()


def deliver(
    answer, residual, relative, answer_out, residual_out, relative_out, held, held_row, sems
):
    def through(source, between, target, i, j):
        return (
            pltpu.make_async_copy(source, between, sems.at[0, i, j]),
            pltpu.make_async_copy(between, target, sems.at[1, i, j]),
        )

    steps = [
        through(source.at[plane], held.at[i, plane], target.at[plane], i, plane)
        for plane in range(L)
        for i, (source, target) in enumerate(((answer, answer_out), (residual, residual_out)))
    ]
    steps.append(through(relative, held_row, relative_out, 2, 0))
    for fetch, _ in steps:
        fetch.start()
    for fetch, store in steps:
        fetch.wait()
        store.start()
    for _, store in steps:
        store.wait()


def local(
    loads, diagonal_blocks, lower_coupling, upper_coupling, local_inverse, deflation,
    coarse_inverse, coarse_order,
):
    hbm = pl.BlockSpec(memory_space=pl.ANY)
    field = pltpu.VMEM((L, K, W), F32)
    padded = pltpu.VMEM((K, (L + 2) * W), BF16)
    blocks = pltpu.VMEM((L, 3, W, W), BF16)
    dma = pltpu.SemaphoreType.DMA
    fields = jax.ShapeDtypeStruct((L, K, W), F32)
    outs = (fields, fields, jax.ShapeDtypeStruct((1, K), F32))
    results = pl.pallas_call(
        kernel,
        out_shape=outs,
        in_specs=[hbm] * 8,
        out_specs=(hbm, hbm, pl.BlockSpec(memory_space=pltpu.VMEM)),
        scratch_shapes=[
            field, field, field, field, field,
            padded, padded, padded, padded,
            blocks, blocks,
            pltpu.VMEM((3 * NDEF, (L + 2) * W), BF16),
            pltpu.VMEM((2, NDEF, W), BF16),
            pltpu.VMEM((2 * 128, L * W), BF16),
            pltpu.VMEM((3 * 128, L * W), BF16),
            pltpu.VMEM((NDEF, 128), F32),
            pltpu.VMEM((NDEF, NCOARSE), F32),
            pltpu.VMEM((NDEF, NCOARSE), F32),
            pltpu.VMEM((4 * NDEF, NCOARSE), BF16),
            pltpu.VMEM((8 * NDEF, SAME), BF16),
            pltpu.VMEM((1, NCOARSE), jnp.int32),
            pltpu.VMEM((1, NCOARSE), jnp.int32),
            pltpu.VMEM((2, SIDE, SIDE, SIDE, NDEF, K), BF16),
            pltpu.VMEM((2, SIDE * NDEF, K), BF16),
            pltpu.VMEM((2, 4 * NDEF, K), F32),
            pltpu.VMEM((2, 3 * NDEF, K), F32),
            pltpu.VMEM((128, K), F32),
            pltpu.VMEM((2, K, 3 * 128), BF16),
            pltpu.VMEM((NDEF, K), F32),
            pltpu.VMEM((K, 128), F32),
            pltpu.VMEM((8, K), F32),
            pltpu.VMEM((3, 8, 8, K), F32),
            dma((L,)), dma((L,)), dma((6,)), dma((2,)), dma((2, L)),
            dma((4, 2)), dma((4, 2)), dma((2, 2, 3, 3)), dma((2, 2, 3, 3)),
            dma((1,)), dma((1,)), dma((2,)), dma((2,)), dma((2,)), dma((2,)),
            dma((2,)), dma((2,)), dma((3, 7)), dma((3, 7)),
        ],
        compiler_params=pltpu.CompilerParams(
            collective_id=0, has_side_effects=True, vmem_limit_bytes=60 * 2**20
        ),
        cost_estimate=pl.CostEstimate(
            flops=8 * 10**9, bytes_accessed=25 * 10**6, transcendentals=0
        ),
    )(
        loads, diagonal_blocks, lower_coupling, upper_coupling, local_inverse, deflation,
        coarse_inverse, coarse_order.reshape(1, NCOARSE),
    )
    answer, residual, ratio = pl.pallas_call(
        deliver,
        out_shape=outs,
        in_specs=[hbm] * 3,
        out_specs=(hbm,) * 3,
        scratch_shapes=[pltpu.VMEM((2, L, K, W), F32), pltpu.VMEM((1, K), F32), dma((2, 3, L))],
        compiler_params=pltpu.CompilerParams(vmem_limit_bytes=60 * 2**20),
    )(*results)
    return answer, residual, ratio.reshape(K)


def solution(mesh):
    spread = P(("grp", "sub"))
    return jax.shard_map(
        local,
        mesh=mesh,
        in_specs=(
            spread, spread, spread, spread, P(None, ("grp", "sub")), spread, spread, P(),
        ),
        out_specs=(spread, spread, P()),
        check_vma=False,
    )
```

```python
import jax
import jax.numpy as jnp
from jax import lax
from jax.experimental import pallas as pl
from jax.experimental.pallas import tpu as pltpu
from jax.sharding import PartitionSpec as P

MESH = pl.DeviceIdType.MESH
F32 = jnp.float32
BF16 = jnp.bfloat16

L = 8
K = 256
W = 384
NDEF = 32
SIDE = 4
DEVICES = 128
SAME = SIDE * SIDE * SIDE * NDEF
NCOARSE = 2 * SAME
BAND = 3 * W
IMAGE_SCALE = 2.0 ** -24
INNER, OUTER = (1, L - 1), (0, 2)
GATHER_PARTS = (("xyz", 0, 16), ("zxy", 16, 32))
NN = (((1,), (0,)), ((), ()))
NT = (((1,), (1,)), ((), ()))


def lanes(plane):
    return pl.ds(pl.multiple_of(plane * W, W), W)


def dot(first, second, form=NN, precision=None):
    return lax.dot_general(
        first, second, form, precision=precision, preferred_element_type=F32
    )


def two_terms(value):
    high = value.astype(BF16)
    return high, (value - high.astype(F32)).astype(BF16)


def kernel(
    loads_h, diagonal_h, lower_h, upper_h, local_h, deflation_h, inverse_h, order_h,
    solution_h, residual_h, relative_ref,
    v0, z0, u0, z1, u1, field0, field1, field2, field3, precond, coupling,
    padded_vectors, edge_vectors, expansion, images, image_coupling,
    own_rows, other_rows, split_rows, columns, order, place, gathered, own_low,
    partial, other_partial, coarse, amounts, projected, gram, sums, slots,
    load_sem, vector_sem, block_sem, row_sem, out_sem,
    halo_send, halo_recv, gather_send, gather_recv, row_send, row_recv,
    edge_send, edge_recv, column_send, column_recv,
    partial_send, partial_recv, sum_send, sum_recv,
):
    grp = lax.axis_index("grp")
    sub = lax.axis_index("sub")
    y, z, x, core = grp // SIDE, grp % SIDE, sub // 2, sub % 2
    me = grp * 8 + sub
    place_of = {"x": x, "y": y, "z": z}

    def along_chain(step):
        device = (me + step + DEVICES) % DEVICES
        return (device // 8, device % 8)

    before_id, after_id = along_chain(-1), along_chain(1)
    chip_before_id, chip_after_id = along_chain(-2), along_chain(2)
    core_id = (grp, x * 2 + 1 - core)

    def chip(at_x, at_y, at_z):
        return (at_y * SIDE + at_z, at_x * 2 + core)

    def partner(axis, step):
        spot = dict(place_of)
        spot[axis] = (spot[axis] + step) % SIDE
        return chip(spot["x"], spot["y"], spot["z"])

    z_low, z_high = z % 2, z // 2
    sum_groups = (
        (z_low * SIDE + x, [
            chip((x + step) % SIDE, y, 2 * z_high + (z_low + flip) % 2)
            for flip in (0, 1) for step in range(SIDE) if flip or step
        ]),
        (z_high * SIDE + y, [
            chip(x, (y + step) % SIDE, 2 * ((z_high + flip) % 2) + z_low)
            for flip in (0, 1) for step in range(SIDE) if flip or step
        ]),
    )

    def load_copy(plane):
        return pltpu.make_async_copy(loads_h.at[plane], v0.at[plane], load_sem.at[plane])

    def vector_copy(plane):
        return pltpu.make_async_copy(
            deflation_h.at[plane], padded_vectors.at[NDEF:2 * NDEF, lanes(plane + 1)],
            vector_sem.at[plane],
        )

    block_copies = [
        pltpu.make_async_copy(source, target, block_sem.at[i])
        for i, (source, target) in enumerate([
            (local_h.at[0], precond.at[:, 0]),
            (local_h.at[1], precond.at[:, 1]),
            (local_h.at[2], precond.at[:, 2]),
            (lower_h, coupling.at[:, 0]),
            (diagonal_h, coupling.at[:, 1]),
            (upper_h, coupling.at[:, 2]),
        ])
    ]
    row_copy = pltpu.make_async_copy(inverse_h, own_rows, row_sem.at[0])
    order_copy = pltpu.make_async_copy(order_h, order, row_sem.at[1])
    for plane in (0, 7, 1, 2, 3, 4, 5, 6):
        load_copy(plane).start()
    for plane in range(L):
        vector_copy(plane).start()
    row_copy.start()
    order_copy.start()

    barrier = pltpu.get_barrier_semaphore()
    outer = (me + DEVICES - 1 + 2 * core) % DEVICES
    partners = [partner(axis, step) for axis in "xyz" for step in (1, 2, 3)]
    partners += [core_id, (outer // 8, outer % 8), chip_before_id, chip_after_id]
    for device in partners:
        pl.semaphore_signal(barrier, inc=1, device_id=device, device_id_type=MESH)

    padded_vectors[:NDEF] = jnp.zeros((NDEF, (L + 2) * W), BF16)
    padded_vectors[2 * NDEF:] = jnp.zeros((NDEF, (L + 2) * W), BF16)
    padded_vectors[NDEF:2 * NDEF, :W] = jnp.zeros((NDEF, W), BF16)
    padded_vectors[NDEF:2 * NDEF, (L + 1) * W:] = jnp.zeros((NDEF, W), BF16)
    expansion[...] = jnp.zeros((2 * 128, L * W), BF16)
    images[...] = jnp.zeros((3 * 128, L * W), BF16)
    columns[4 * NDEF:5 * NDEF] = jnp.zeros((NDEF, SAME), BF16)
    columns[7 * NDEF:] = jnp.zeros((NDEF, SAME), BF16)
    own_low[...] = jnp.zeros((2, SIDE * NDEF, K), BF16)
    gram[...] = jnp.zeros((K, 128), F32)
    projected[...] = jnp.zeros((NDEF, K), F32)
    coarse[...] = jnp.zeros((128, K), F32)

    sends = []

    def remote(source, target, send, recv, device):
        return pltpu.make_async_remote_copy(
            src_ref=source, dst_ref=target, send_sem=send, recv_sem=recv,
            device_id=device, device_id_type=MESH,
        )

    def start(copies):
        for copy in copies:
            copy.start()
        sends.extend(copies)

    def received(copies):
        for copy in copies:
            copy.wait_recv()

    row_exchange = [
        remote(inverse_h, other_rows, row_send.at[0], row_recv.at[0], core_id)
    ]
    edge_exchange = [
        remote(
            deflation_h.at[0], edge_vectors.at[1], edge_send.at[0], edge_recv.at[0], before_id
        ),
        remote(
            deflation_h.at[L - 1], edge_vectors.at[0], edge_send.at[1], edge_recv.at[1], after_id
        ),
    ]
    column_exchange = [
        remote(
            columns.at[row:row + NDEF], columns.at[target:target + NDEF],
            column_send.at[i], column_recv.at[i], device,
        )
        for i, (row, target, device) in enumerate([
            (2 * NDEF, 0, chip_after_id),
            (NDEF, 3 * NDEF, chip_before_id),
        ])
    ]

    def halo_copies(field, which):
        return [
            remote(
                field.at[:, lanes(1)], field.at[:, lanes(L + 1)],
                halo_send.at[which, 0], halo_recv.at[which, 0], before_id,
            ),
            remote(
                field.at[:, lanes(L)], field.at[:, lanes(0)],
                halo_send.at[which, 1], halo_recv.at[which, 1], after_id,
            ),
        ]

    def start_halo(field, which):
        start(halo_copies(field, which))

    def finish_halo(field, which):
        received(halo_copies(field, which))

        @pl.when(me == 0)
        def _():
            field[:, lanes(0)] = jnp.zeros((K, W), BF16)

        @pl.when(me == DEVICES - 1)
        def _():
            field[:, lanes(L + 1)] = jnp.zeros((K, W), BF16)

    def gather_copies(which, stage):
        found = []
        for part, (axes, row0, row1) in enumerate(GATHER_PARTS):
            done = axes[:stage]
            spot = tuple(slice(None) if name in done else place_of[name] for name in "yzx")
            block = gathered.at[(which,) + spot + (slice(row0, row1),)]
            for step in (1, 2, 3):
                found.append(remote(
                    block, block,
                    gather_send.at[which, part, stage, step - 1],
                    gather_recv.at[which, part, stage, step - 1],
                    partner(axes[stage], step),
                ))
        return found

    def start_gather(which, stage):
        start(gather_copies(which, stage))

    def finish_gather(which, stage):
        received(gather_copies(which, stage))

    def share_coefficients(own, which):
        high, low = two_terms(own)
        gathered[which, y, z, x] = high
        start_gather(which, 0)
        own_low[which, pl.ds(pl.multiple_of(x * NDEF, NDEF), NDEF)] = low

    def banded(field, blocks, plane):
        window = field[:, pl.ds(pl.multiple_of(plane * W, W), BAND)]
        return dot(window, blocks[plane].reshape(BAND, W))

    def edge(i):
        return i * (L - 1)

    def finish_coarse(which):
        product = dot(columns[...], gathered[which].reshape(SAME, K))
        window = pl.ds(pl.multiple_of((y * SIDE + z) * 128, 128), 128)
        fix = dot(columns[:4 * NDEF, window], own_low[which])
        partial[which] = product[:4 * NDEF] + (product[4 * NDEF:] + fix)
        exchange = [remote(
            partial.at[which, pl.ds(pl.multiple_of((1 - core) * NDEF, NDEF), 3 * NDEF)],
            other_partial.at[which], partial_send.at[which], partial_recv.at[which], core_id,
        )]
        start(exchange)
        received(exchange)
        coarse[:3 * NDEF] = (
            partial[which, pl.ds(pl.multiple_of(core * NDEF, NDEF), 3 * NDEF)]
            + other_partial[which]
        )
        high, low = two_terms(jnp.transpose(coarse[...]))
        amounts[which, :, :128] = high
        amounts[which, :, 128:256] = low
        amounts[which, :, 256:] = high

    def precondition(field, result, rounded, planes):
        @pl.loop(*planes)
        def _(i):
            plane = i if planes == INNER else edge(i)
            value = banded(field, precond, plane)
            result[plane] = value
            rounded[:, lanes(plane + 1)] = value.astype(BF16)

    def operate(field, result, planes, project):
        @pl.loop(*planes)
        def _(i):
            plane = i if planes == INNER else edge(i)
            image = banded(field, coupling, plane)
            result[plane] = image
            if project:
                projected[...] += dot(
                    padded_vectors[NDEF:2 * NDEF, lanes(plane + 1)], image.astype(BF16), NT
                )

    def add_image(result, rounded, plane, which):
        total = result[plane] + dot(amounts[which], images[:, lanes(plane)])
        result[plane] = total
        if rounded is not None:
            rounded[:, lanes(plane + 1)] = total.astype(BF16)

    def add_expansion(result, which):
        @pl.loop(0, L)
        def _(plane):
            result[plane] += dot(amounts[which, :, :256], expansion[:, lanes(plane)])

    def inner_products(fields, pairs):
        rows = 32

        @pl.loop(0, K // rows)
        def _(chunk):
            span = pl.ds(pl.multiple_of(chunk * rows, rows), rows)
            totals = [jnp.zeros((rows, 128), F32) for _ in pairs]
            for plane in range(L):
                for lane in range(0, W, 128):
                    values = [field[plane, span, lane:lane + 128] for field in fields]
                    if len(values) == 3:
                        values[2] = values[2] * IMAGE_SCALE
                    totals = [
                        total + values[first] * values[second]
                        for total, (_, first, second) in zip(totals, pairs)
                    ]
            for total, (column, _, _) in zip(totals, pairs):
                gram[span, column:column + 1] = jnp.sum(total, axis=1, keepdims=True)

    def permute_columns(first, last):
        @pl.loop(first, last)
        def _(block):
            base = block * 256
            total = jnp.zeros((256, 4 * NDEF), F32)
            for part in range(4):
                span = slice(part * 1024, (part + 1) * 1024)
                spot = place[:, span] - base
                inside = (spot >= 0) & (spot < 256)
                spot = jnp.where(inside, spot, -1).astype(F32).astype(BF16)
                row = lax.broadcasted_iota(jnp.int32, (256, 1024), 0).astype(F32).astype(BF16)
                hot = jnp.where(spot == row, jnp.ones((), BF16), jnp.zeros((), BF16))
                total += dot(hot, split_rows[:, span], NT)
            total = jnp.transpose(total).astype(BF16)
            target = pl.ds(pl.multiple_of(base, 256), 256)
            columns[NDEF:3 * NDEF, target] = total[:2 * NDEF]
            columns[5 * NDEF:7 * NDEF, target] = total[2 * NDEF:]

    for plane in (0, 7, 1, 2, 3, 4, 5, 6):
        load_copy(plane).wait()
        field0[:, lanes(plane + 1)] = v0[plane].astype(BF16)

    for plane in range(L):
        vector_copy(plane).wait()
    for copy in block_copies:
        copy.start()
    first_coefficients = dot(
        padded_vectors[NDEF:2 * NDEF, W:(L + 1) * W], field0[:, W:(L + 1) * W], NT
    )
    pl.semaphore_wait(barrier, len(partners))
    share_coefficients(first_coefficients, 0)
    start(row_exchange)
    start_halo(field0, 0)
    start(edge_exchange)

    row_copy.wait()
    order_copy.wait()
    received(row_exchange)
    for rows, owner in ((own_rows, core), (other_rows, 1 - core)):
        high, low = two_terms(rows[...])
        split_rows[pl.ds(pl.multiple_of(owner * NDEF, NDEF), NDEF)] = high
        split_rows[pl.ds(pl.multiple_of((2 + owner) * NDEF, NDEF), NDEF)] = low
    unknown = order[...]
    inside = unknown % (2 * NDEF)
    place[...] = jnp.where(
        inside // NDEF == core, unknown // (2 * NDEF) * NDEF + inside % NDEF, -1
    )
    permute_columns(0, 4)
    finish_gather(0, 0)
    start_gather(0, 1)
    permute_columns(4, SAME // 256)
    start(column_exchange)
    finish_gather(0, 1)
    start_gather(0, 2)

    for copy in block_copies[:3]:
        copy.wait()
    finish_halo(field0, 0)
    precondition(field0, z0, field1, OUTER)
    start_halo(field1, 1)
    precondition(field0, z0, field1, INNER)
    for copy in block_copies[3:]:
        copy.wait()
    operate(field1, u0, INNER, True)
    received(edge_exchange)
    padded_vectors[:NDEF, :W] = jnp.where(me > 0, edge_vectors[0], 0)
    padded_vectors[2 * NDEF:, (L + 1) * W:] = jnp.where(me < DEVICES - 1, edge_vectors[1], 0)

    @pl.loop(0, L)
    def _(plane):
        high, low = two_terms(banded(padded_vectors, coupling, plane))
        images[:3 * NDEF, lanes(plane)] = high
        images[128:128 + 3 * NDEF, lanes(plane)] = high
        images[256:256 + 3 * NDEF, lanes(plane)] = low
        own = padded_vectors[NDEF:2 * NDEF, lanes(plane + 1)]
        expansion[NDEF:2 * NDEF, lanes(plane)] = own
        expansion[128 + NDEF:128 + 2 * NDEF, lanes(plane)] = own

    vectors = padded_vectors[NDEF:2 * NDEF, W:(L + 1) * W]
    image_coupling[...] = dot(vectors, images[:128], NT) + dot(vectors, images[256:], NT)
    finish_halo(field1, 1)
    operate(field1, u0, OUTER, True)
    finish_gather(0, 2)
    received(column_exchange)
    finish_coarse(0)
    share_coefficients(
        projected[...] + dot(image_coupling[...], coarse[...], NN, lax.Precision.HIGHEST), 1
    )

    @pl.loop(0, 2)
    def _(i):
        add_image(u0, field2, edge(i), 0)

    start_halo(field2, 2)

    @pl.loop(1, L - 1)
    def _(plane):
        add_image(u0, field2, plane, 0)

    finish_gather(1, 0)
    start_gather(1, 1)
    inner_products((v0, u0), ((0, 0, 0), (1, 0, 1), (2, 1, 1)))
    precondition(field2, z1, field3, INNER)
    finish_gather(1, 1)
    start_gather(1, 2)
    finish_halo(field2, 2)
    precondition(field2, z1, field3, OUTER)
    start_halo(field3, 3)
    operate(field3, u1, INNER, False)
    add_expansion(z0, 0)
    finish_halo(field3, 3)
    operate(field3, u1, OUTER, False)
    finish_gather(1, 2)
    finish_coarse(1)

    @pl.loop(0, L)
    def _(plane):
        add_image(u1, None, plane, 1)

    inner_products((v0, u0, u1), ((3, 0, 2), (4, 1, 2), (5, 2, 2)))
    sums[...] = jnp.transpose(gram[...])[:8]

    pair = remote(sums, slots.at[0, 0], sum_send.at[0, 0], sum_recv.at[0, 0], core_id)
    pair.start()
    pair.wait()
    sums[...] = sums[...] + slots[0, 0]
    for stage, (spot, group) in enumerate(sum_groups):
        slots[1 + stage, spot] = sums[...]
        copies = [
            remote(
                slots.at[1 + stage, spot], slots.at[1 + stage, spot],
                sum_send.at[1 + stage, i], sum_recv.at[1 + stage, i], device,
            )
            for i, device in enumerate(group)
        ]
        for copy in copies:
            copy.start()
        if stage == 0:
            add_expansion(z1, 1)
        for copy in copies:
            copy.wait()
        sums[...] = (
            ((slots[1 + stage, 0] + slots[1 + stage, 1])
             + (slots[1 + stage, 2] + slots[1 + stage, 3]))
            + ((slots[1 + stage, 4] + slots[1 + stage, 5])
               + (slots[1 + stage, 6] + slots[1 + stage, 7]))
        )

    g00, g01, g11 = sums[0:1], sums[1:2], sums[2:3]
    g02, g12, g22 = sums[3:4], sums[4:5], sums[5:6]
    s0, s1, s2 = jnp.sqrt(g00), jnp.sqrt(g11), jnp.sqrt(g22)
    r01 = g01 / s0 / s1
    r02 = g02 / s0 / s2
    r11 = jnp.sqrt((1.0 - r01) * (1.0 + r01))
    r12 = (g12 / s1 / s2 - r01 * r02) / r11
    r22 = jnp.sqrt((1.0 - r02) * (1.0 + r02) - r12 * r12)
    n0 = r11 * r22
    n1 = r01 * r22
    n2 = r01 * r12 - r11 * r02
    share = n0 / (n0 * n0 + n1 * n1 + n2 * n2)
    relative_ref[...] = n0 * share
    scaled1 = -(share * n2) / r22
    weight1 = scaled1 * (s0 / s2) * IMAGE_SCALE
    weight0 = (share * n1 - scaled1 * r12) / r11 * (s0 / s1)
    gram[...] = jnp.transpose(
        jnp.concatenate([weight0, weight1, jnp.zeros((126, K), F32)], axis=0)
    )

    def solution_copy(plane):
        return pltpu.make_async_copy(z0.at[plane], solution_h.at[plane], out_sem.at[0, plane])

    def residual_copy(plane):
        return pltpu.make_async_copy(v0.at[plane], residual_h.at[plane], out_sem.at[1, plane])

    @pl.loop(0, L)
    def _(plane):
        first, second = gram[:, 0:1], gram[:, 1:2]
        z0[plane] = first * z0[plane] + second * z1[plane]
        solution_copy(plane).start()
        v0[plane] = v0[plane] - first * u0[plane] - second * u1[plane]
        residual_copy(plane).start()

    for copy in sends:
        copy.wait_send()

    @pl.loop(0, L)
    def _(plane):
        solution_copy(plane).wait()
        residual_copy(plane).wait()


def deliver(
    answer, residual, relative, answer_out, residual_out, relative_out, held, held_row, sems
):
    def through(source, between, target, i, j):
        return (
            pltpu.make_async_copy(source, between, sems.at[0, i, j]),
            pltpu.make_async_copy(between, target, sems.at[1, i, j]),
        )

    steps = [
        through(source.at[plane], held.at[i, plane], target.at[plane], i, plane)
        for plane in range(L)
        for i, (source, target) in enumerate(((answer, answer_out), (residual, residual_out)))
    ]
    steps.append(through(relative, held_row, relative_out, 2, 0))
    for fetch, _ in steps:
        fetch.start()
    for fetch, store in steps:
        fetch.wait()
        store.start()
    for _, store in steps:
        store.wait()


def local(
    loads, diagonal_blocks, lower_coupling, upper_coupling, local_inverse, deflation,
    coarse_inverse, coarse_order,
):
    hbm = pl.BlockSpec(memory_space=pl.ANY)
    field = pltpu.VMEM((L, K, W), F32)
    padded = pltpu.VMEM((K, (L + 2) * W), BF16)
    blocks = pltpu.VMEM((L, 3, W, W), BF16)
    dma = pltpu.SemaphoreType.DMA
    fields = jax.ShapeDtypeStruct((L, K, W), F32)
    outs = (fields, fields, jax.ShapeDtypeStruct((1, K), F32))
    results = pl.pallas_call(
        kernel,
        out_shape=outs,
        in_specs=[hbm] * 8,
        out_specs=(hbm, hbm, pl.BlockSpec(memory_space=pltpu.VMEM)),
        scratch_shapes=[
            field, field, field, field, field,
            padded, padded, padded, padded,
            blocks, blocks,
            pltpu.VMEM((3 * NDEF, (L + 2) * W), BF16),
            pltpu.VMEM((2, NDEF, W), BF16),
            pltpu.VMEM((2 * 128, L * W), BF16),
            pltpu.VMEM((3 * 128, L * W), BF16),
            pltpu.VMEM((NDEF, 128), F32),
            pltpu.VMEM((NDEF, NCOARSE), F32),
            pltpu.VMEM((NDEF, NCOARSE), F32),
            pltpu.VMEM((4 * NDEF, NCOARSE), BF16),
            pltpu.VMEM((8 * NDEF, SAME), BF16),
            pltpu.VMEM((1, NCOARSE), jnp.int32),
            pltpu.VMEM((1, NCOARSE), jnp.int32),
            pltpu.VMEM((2, SIDE, SIDE, SIDE, NDEF, K), BF16),
            pltpu.VMEM((2, SIDE * NDEF, K), BF16),
            pltpu.VMEM((2, 4 * NDEF, K), F32),
            pltpu.VMEM((2, 3 * NDEF, K), F32),
            pltpu.VMEM((128, K), F32),
            pltpu.VMEM((2, K, 3 * 128), BF16),
            pltpu.VMEM((NDEF, K), F32),
            pltpu.VMEM((K, 128), F32),
            pltpu.VMEM((8, K), F32),
            pltpu.VMEM((3, 8, 8, K), F32),
            dma((L,)), dma((L,)), dma((6,)), dma((2,)), dma((2, L)),
            dma((4, 2)), dma((4, 2)), dma((2, 2, 3, 3)), dma((2, 2, 3, 3)),
            dma((1,)), dma((1,)), dma((2,)), dma((2,)), dma((2,)), dma((2,)),
            dma((2,)), dma((2,)), dma((3, 7)), dma((3, 7)),
        ],
        compiler_params=pltpu.CompilerParams(
            collective_id=0, has_side_effects=True, vmem_limit_bytes=60 * 2**20
        ),
        cost_estimate=pl.CostEstimate(
            flops=8 * 10**9, bytes_accessed=25 * 10**6, transcendentals=0
        ),
    )(
        loads, diagonal_blocks, lower_coupling, upper_coupling, local_inverse, deflation,
        coarse_inverse, coarse_order.reshape(1, NCOARSE),
    )
    answer, residual, ratio = pl.pallas_call(
        deliver,
        out_shape=outs,
        in_specs=[hbm] * 3,
        out_specs=(hbm,) * 3,
        scratch_shapes=[pltpu.VMEM((2, L, K, W), F32), pltpu.VMEM((1, K), F32), dma((2, 3, L))],
        compiler_params=pltpu.CompilerParams(vmem_limit_bytes=60 * 2**20),
    )(*results)
    return answer, residual, ratio.reshape(K)


def solution(mesh):
    spread = P(("grp", "sub"))
    return jax.shard_map(
        local,
        mesh=mesh,
        in_specs=(
            spread, spread, spread, spread, P(None, ("grp", "sub")), spread, spread, P(),
        ),
        out_specs=(spread, spread, P()),
        check_vma=False,
    )
```
